256 devices in a mesh: slab: 8 (over z), col: 32 (over x, y, core).
Axes of the slice: x: 4, y: 4, z: 8, core: 2. Of those that a mesh axis runs over, the one named last changes fastest.
Arguments:
- tensor: float32 [128, 2048, 2048], P('slab', 'col')
- signs3: int32 [2048], replicated, may hold values from -1 to 1, as said below
- picked3: int32 [256], replicated, may hold values from 0 to 2047, as said below
- signs2: int32 [2048], replicated, may hold values from -1 to 1, as said below
- picked2: int32 [256], replicated, may hold values from 0 to 2047, as said below
Outputs:
- basis: float32 [256, 128, 256], P('col', 'slab')
The draws below stay inside these ranges and needn't reach their ends.
Inputs may be any that keep to these rules, and one draw needn't show every extreme that they name: `signs3`: each entry is -1 or 1. `signs2`: each entry is -1 or 1. `picked3`: distinct and increasing; 0 and 2047 are always among them. `picked2`: distinct and increasing; 0 and 2047 are always among them.
All inputs are finite; a program needn't handle non-finite values.
Results may differ from the reference program's by a relative error of at most 0.0003.
Values sent between devices are 32-bit elements; how exact they have to be, the bound alone decides.
A program may use at most 64 MiB of HBM per device.

```python
import math
import jax
import jax.numpy as jnp
from jax import lax

N3 = 2048
N2 = 2048
R3 = 256
R2 = 256
N1 = 128


def picked_rows(key, length, count):
    inner = jax.random.permutation(key, length - 2)[:count - 2] + 1
    ends = jnp.array([0, length - 1], dtype=jnp.int32)
    return jnp.sort(jnp.concatenate([inner.astype(jnp.int32), ends]))


def draw_tensor(key, part):
    key = jax.random.fold_in(key, 11)
    first, second, third = jax.random.split(key, 3)
    row_scale = jnp.exp(jax.random.uniform(first, (N1, 1, 1), jnp.float32) * math.log(10.0))
    ramp = jnp.arange(N2, dtype=jnp.float32) / (N2 - 1)
    col_scale = jnp.exp(ramp * math.log(3.0)).reshape(1, N2, 1)
    col_scale = col_scale * jnp.exp(jax.random.uniform(second, (1, N2, 1), jnp.float32) * math.log(2.0))
    base = jax.random.normal(third, (N1, N2, N3), jnp.float32)
    return (base * row_scale * col_scale).astype(jnp.float32)


def draw_signs3(key, part):
    key = jax.random.fold_in(key, 23)
    return (2 * jax.random.randint(key, (N3,), 0, 2) - 1).astype(jnp.int32)


def draw_signs2(key, part):
    key = jax.random.fold_in(key, 37)
    return (2 * jax.random.randint(key, (N2,), 0, 2) - 1).astype(jnp.int32)


def draw_picked3(key, part):
    key = jax.random.fold_in(key, 41)
    return picked_rows(key, N3, R3)


def draw_picked2(key, part):
    key = jax.random.fold_in(key, 53)
    return picked_rows(key, N2, R2)


def setup_inputs(seed: int = 0) -> dict:
    splits = jax.random.split(jax.random.key(seed), 6)
    return {
        "tensor": draw_tensor(jax.random.fold_in(splits[5], 71), 0),
        "signs3": draw_signs3(jax.random.fold_in(splits[5], 71), 0),
        "picked3": draw_picked3(jax.random.fold_in(splits[5], 71), 0),
        "signs2": draw_signs2(jax.random.fold_in(splits[5], 71), 0),
        "picked2": draw_picked2(jax.random.fold_in(splits[5], 71), 0),
    }


def hadamard_rows(picked, columns, bits):
    parity = jnp.zeros((picked.shape[0], columns.shape[0]), jnp.int32)
    for place in range(bits):
        upper = jnp.bitwise_and(jnp.right_shift(picked, place), 1)
        lower = jnp.bitwise_and(jnp.right_shift(columns, place), 1)
        parity = parity + upper[:, None] * lower[None, :]
    return (1 - 2 * (parity % 2)).astype(jnp.float32)

def reference(tensor, signs3, picked3, signs2, picked2):
    table3 = hadamard_rows(picked3, jnp.arange(N3, dtype=jnp.int32), N3.bit_length() - 1)
    table3 = table3 * signs3.astype(jnp.float32)[None, :]
    table2 = hadamard_rows(picked2, jnp.arange(N2, dtype=jnp.int32), N2.bit_length() - 1)
    table2 = table2 * signs2.astype(jnp.float32)[None, :]

    def one_slice(plane):
        first = jnp.dot(plane.astype(jnp.float32), table3.T.astype(jnp.float32), precision=lax.Precision.HIGHEST, preferred_element_type=jnp.float32)
        return jnp.dot(table2.astype(jnp.float32), first.astype(jnp.float32), precision=lax.Precision.HIGHEST, preferred_element_type=jnp.float32)
    sketch = lax.map(one_slice, tensor)
    flat = sketch.reshape(N1, R2 * R3)
    gram = jnp.dot(flat.astype(jnp.float32), flat.T.astype(jnp.float32), precision=lax.Precision.HIGHEST, preferred_element_type=jnp.float32)
    lower = jnp.linalg.cholesky(gram)
    identity = jnp.eye(N1, dtype=jnp.float32)
    inverse = lax.linalg.triangular_solve(lower, identity, left_side=True, lower=True)
    basis = jnp.dot(inverse.astype(jnp.float32), flat.astype(jnp.float32), precision=lax.Precision.HIGHEST, preferred_element_type=jnp.float32)
    basis = basis * jnp.float32((R2 * R3) ** 0.5)
    return basis.reshape(N1, R2, R3).transpose(1, 0, 2)
```

```python
import jax
import jax.numpy as jnp
from jax import lax
from jax.experimental import pallas as pl
from jax.experimental.pallas import tpu as pltpu
from jax.sharding import PartitionSpec as P

MESH = pl.DeviceIdType.MESH
SIDE = 4
CHIPS = SIDE * SIDE
CORES = 2
COLS = CHIPS * CORES
SLABS = 8
WIDTH = 64
LENGTH = 2048
RANK = 256
HALF = 128
ROWS = SLABS * CHIPS
BLOCK = 8
F32 = jnp.float32
BF16 = jnp.bfloat16


def split_two(value):
    high = value.astype(BF16)
    return high, (value - high.astype(F32)).astype(BF16)


def split_three(value):
    high = value.astype(BF16)
    rest = value - high.astype(F32)
    middle = rest.astype(BF16)
    return high, middle, (rest - middle.astype(F32)).astype(BF16)


def exact_dot(left, right, dims):
    lh, lm, ll = split_three(left)
    rh, rm, rl = split_three(right)
    (la,), (ra,) = dims
    return lax.dot_general(
        jnp.concatenate([lh, lh, lm, lm, lh, ll], axis=la),
        jnp.concatenate([rh, rm, rh, rm, rl, rh], axis=ra),
        (dims, ((), ())),
        preferred_element_type=F32,
    )


def odd(value):
    value = value ^ (value >> 8)
    value = value ^ (value >> 4)
    value = value ^ (value >> 2)
    value = value ^ (value >> 1)
    return (1 - 2 * (value & 1)).astype(F32)


def inverse_factor(held):
    lane = lax.broadcasted_iota(jnp.int32, (BLOCK, ROWS), 1)
    sub = lax.broadcasted_iota(jnp.int32, (BLOCK, ROWS), 0)
    for base in range(0, ROWS, BLOCK):
        rows = [
            jnp.broadcast_to(held[base + i : base + i + 1, :], (BLOCK, ROWS)) for i in range(BLOCK)
        ]
        cell = {}
        for i in range(BLOCK):
            for j in range(i + 1):
                cell[i, j] = jnp.broadcast_to(rows[i][:, base + j : base + j + 1], (BLOCK, ROWS))
        own = jnp.logical_and(lane >= base, lane < base + BLOCK)
        rows = [
            jnp.where(own, jnp.where(lane == base + i, F32(1), F32(0)), rows[i])
            for i in range(BLOCK)
        ]
        for k in range(BLOCK):
            root = lax.rsqrt(cell[k, k])
            rows[k] = rows[k] * root
            for i in range(k + 1, BLOCK):
                cell[i, k] = cell[i, k] * root
            for i in range(k + 1, BLOCK):
                for j in range(k + 1, i + 1):
                    cell[i, j] = cell[i, j] - cell[i, k] * cell[j, k]
                rows[i] = rows[i] - cell[i, k] * rows[k]
        tile = rows[0]
        for i in range(1, BLOCK):
            tile = jnp.where(sub == i, rows[i], tile)
        held[base : base + BLOCK, :] = tile
        if base + BLOCK < ROWS:
            update = exact_dot(tile, tile, ((0,), (0,)))
            rest = held[base + BLOCK :, :]
            clear = lax.broadcasted_iota(jnp.int32, rest.shape, 1)
            clear = jnp.logical_and(clear >= base, clear < base + BLOCK)
            held[base + BLOCK :, :] = jnp.where(clear, F32(0), rest) - update[base + BLOCK :, :]


def kernel(
    tensor, signs3, picked3, signs2, picked2, out,
    slabs, table3, table2, outgoing, landed, sketch, spread, slices, planes,
    partial_gram, terms, row_block, blocks, block, gram, result, returned,
    load_sem, send_sem, recv_sem, spread_send, spread_recv, slice_send, slice_recv,
    term_send, term_recv, block_send, block_recv, gram_send, gram_recv, back_send, back_recv,
):
    z = lax.axis_index("slab")
    p = lax.axis_index("col")
    q = p // CORES
    h = p % CORES
    x, y = q // SIDE, q % SIDE

    def shifted(step, sign):
        turn = (step + 1) % CHIPS
        dx, dy = turn // SIDE, turn % SIDE
        return ((x + sign * dx + SIDE) % SIDE) * SIDE + (y + sign * dy + SIDE) % SIDE

    def load(step):
        return pltpu.make_async_copy(tensor.at[shifted(step, 1)], slabs.at[step], load_sem.at[step])

    @pl.loop(0, CHIPS)
    def _(step):
        load(step).start()

    barrier = pltpu.get_barrier_semaphore()

    @pl.loop(1, COLS)
    def _(step):
        pl.semaphore_signal(barrier, 1, device_id=(z, (p + step) % COLS), device_id_type=MESH)

    @pl.loop(1, SLABS)
    def _(step):
        for core in range(CORES):
            pl.semaphore_signal(
                barrier, 1, device_id=((z + step) % SLABS, q * CORES + core), device_id_type=MESH
            )

    below = lax.broadcasted_iota(jnp.int32, (HALF, HALF), 0)
    for half in range(RANK // HALF):
        picks = picked3[half : half + 1, :]
        low = odd(below & jnp.broadcast_to(picks, (HALF, HALF)))
        for tile in range(LENGTH // HALF):
            high = odd(jnp.broadcast_to(picks, (BLOCK, HALF)) & (tile * HALF))[:1]
            table3[tile * HALF : (tile + 1) * HALF, half * HALF : (half + 1) * HALF] = (
                low * high
            ).astype(BF16)
    along = lax.broadcasted_iota(jnp.int32, (HALF, HALF), 1)
    for half in range(RANK // HALF):
        picks = picked2[half : half + 1, :].astype(F32)
        picks = jnp.broadcast_to(picks, (HALF, HALF)).T.astype(jnp.int32)
        low = odd(along & picks)
        for tile in range(CHIPS):
            high = odd(picks & (tile * HALF))
            signs = signs2[tile : tile + 1, :].astype(F32)
            table2[tile, half * HALF : (half + 1) * HALF, :] = (low * high * signs).astype(BF16)

    pl.semaphore_wait(barrier, COLS - 1 + (SLABS - 1) * CORES)

    def piece(step, core):
        chip = shifted(step, 1)
        return pltpu.make_async_remote_copy(
            outgoing.at[step, core],
            landed.at[p],
            send_sem.at[step, core],
            recv_sem.at[p],
            device_id=(z, chip * CORES + core),
            device_id_type=MESH,
        )

    @pl.loop(0, CHIPS, step=2)
    def _(step):
        load(step).wait()
        load(step + 1).wait()
        both = slabs[pl.ds(step, 2)].reshape(2 * WIDTH, LENGTH)
        highs, lows = [], []
        for tile in range(LENGTH // HALF):
            signs = signs3[tile : tile + 1, :].astype(F32)
            high, low = split_two(both[:, tile * HALF : (tile + 1) * HALF] * signs)
            highs.append(high)
            lows.append(low)
        left = jnp.concatenate(
            [jnp.concatenate(highs, axis=1), jnp.concatenate(lows, axis=1)], axis=0
        )
        first = jnp.dot(left, table3[...], preferred_element_type=F32)
        first = first[: 2 * WIDTH] + first[2 * WIDTH :]
        for part in range(2):
            for core in range(CORES):
                outgoing[step + part, core] = first[
                    part * WIDTH : (part + 1) * WIDTH, core * HALF : (core + 1) * HALF
                ]
        for core in range(CORES):
            piece(step, core).start()

        @pl.when(step + 1 < CHIPS - 1)
        def _():
            for core in range(CORES):
                piece(step + 1, core).start()

        @pl.when(step + 1 == CHIPS - 1)
        def _():
            piece(step + 1, 1 - h).start()

    landed[p] = outgoing[CHIPS - 1, h]

    def arrival(source):
        return pltpu.make_async_remote_copy(
            outgoing.at[0, 0],
            landed.at[source],
            send_sem.at[0, 0],
            recv_sem.at[source],
            device_id=(z, p ^ 1),
            device_id_type=MESH,
        )

    def two_chips(step, total):
        lefts, rights = [], []
        for part in range(2):
            chip = shifted(step + part, -1)

            @pl.when(step + part < CHIPS - 1)
            def _():
                for core in range(CORES):
                    arrival(chip * CORES + core).wait_recv()

            @pl.when(step + part == CHIPS - 1)
            def _():
                arrival(p ^ 1).wait_recv()

            lefts.append(table2[chip])
            value = landed[pl.ds(chip * CORES, CORES)].reshape(CORES * WIDTH, HALF)
            rights.append(jnp.concatenate(split_two(value), axis=1))
        return total + jnp.dot(
            jnp.concatenate(lefts, axis=1),
            jnp.concatenate(rights, axis=0),
            preferred_element_type=F32,
        )

    total = lax.fori_loop(
        0, CHIPS // 2, lambda n, t: two_chips(2 * n, t), jnp.zeros((RANK, 2 * HALF), F32)
    )
    sketch[...] = (total[:, :HALF] + total[:, HALF:]).reshape(COLS, RANK // COLS, HALF)

    def row_copy(step):
        to = (p + step) % COLS
        return pltpu.make_async_remote_copy(
            sketch.at[to],
            spread.at[q, h],
            spread_send.at[step],
            spread_recv.at[p],
            device_id=(z, to),
            device_id_type=MESH,
        )

    def row_arrival(step):
        source = (p + step) % COLS
        return pltpu.make_async_remote_copy(
            sketch.at[source],
            spread.at[source // CORES, source % CORES],
            spread_send.at[step],
            spread_recv.at[source],
            device_id=(z, source),
            device_id_type=MESH,
        )

    @pl.loop(1, COLS)
    def _(step):
        row_copy(step).start()

    spread[q, h] = sketch[p]

    @pl.loop(1, COLS)
    def _(step):
        row_arrival(step).wait_recv()

    for core in range(CORES):
        for r in range(SLABS):
            slices[r, :, core * HALF : (core + 1) * HALF] = spread[:, core, r, :]

    def slice_copy(step):
        to = (z + step) % SLABS
        return pltpu.make_async_remote_copy(
            slices.at[to],
            planes.at[z],
            slice_send.at[step],
            slice_recv.at[z],
            device_id=(to, p),
            device_id_type=MESH,
        )

    def slice_arrival(step):
        source = (z + step) % SLABS
        return pltpu.make_async_remote_copy(
            slices.at[source],
            planes.at[source],
            slice_send.at[step],
            slice_recv.at[source],
            device_id=(source, p),
            device_id_type=MESH,
        )

    @pl.loop(1, SLABS)
    def _(step):
        slice_copy(step).start()

    planes[z] = slices[z]

    @pl.loop(1, SLABS)
    def _(step):
        slice_arrival(step).wait_recv()

    flat = planes[...].reshape(ROWS, RANK)
    partial_gram[...] = exact_dot(flat, flat, ((1,), (1,))).reshape(CHIPS, BLOCK, ROWS)

    def term_copy(step):
        to = (q + step) % CHIPS
        return pltpu.make_async_remote_copy(
            partial_gram.at[to],
            terms.at[q],
            term_send.at[step],
            term_recv.at[q],
            device_id=(z, to * CORES + h),
            device_id_type=MESH,
        )

    def term_arrival(step):
        source = (q + step) % CHIPS
        return pltpu.make_async_remote_copy(
            partial_gram.at[source],
            terms.at[source],
            term_send.at[step],
            term_recv.at[source],
            device_id=(z, source * CORES + h),
            device_id_type=MESH,
        )

    @pl.loop(1, CHIPS)
    def _(step):
        term_copy(step).start()

    terms[q] = partial_gram[q]

    @pl.loop(1, CHIPS)
    def _(step):
        term_arrival(step).wait_recv()

    row_block[...] = jnp.sum(terms[...], axis=0)

    place = z * CORES + h
    places = SLABS * CORES

    def block_copy(step):
        to = (place + step) % places
        return pltpu.make_async_remote_copy(
            row_block,
            blocks.at[place],
            block_send.at[step],
            block_recv.at[place],
            device_id=(to // CORES, q * CORES + to % CORES),
            device_id_type=MESH,
        )

    def block_arrival(step):
        source = (place + step) % places
        return pltpu.make_async_remote_copy(
            row_block,
            blocks.at[source],
            block_send.at[step],
            block_recv.at[source],
            device_id=(source // CORES, q * CORES + source % CORES),
            device_id_type=MESH,
        )

    @pl.loop(1, places)
    def _(step):
        block_copy(step).start()

    blocks[place] = row_block[...]

    @pl.loop(1, places)
    def _(step):
        block_arrival(step).wait_recv()

    block[...] = jnp.sum(blocks[...], axis=0)

    def gram_copy(step):
        to = (q + step) % CHIPS
        return pltpu.make_async_remote_copy(
            block,
            gram.at[pl.ds(q * BLOCK, BLOCK)],
            gram_send.at[step],
            gram_recv.at[q],
            device_id=(z, to * CORES + h),
            device_id_type=MESH,
        )

    def gram_arrival(step):
        source = (q + step) % CHIPS
        return pltpu.make_async_remote_copy(
            block,
            gram.at[pl.ds(source * BLOCK, BLOCK)],
            gram_send.at[step],
            gram_recv.at[source],
            device_id=(z, source * CORES + h),
            device_id_type=MESH,
        )

    @pl.loop(1, CHIPS)
    def _(step):
        gram_copy(step).start()

    gram[pl.ds(pl.multiple_of(q * BLOCK, BLOCK), BLOCK), :] = block[...]

    @pl.loop(1, CHIPS)
    def _(step):
        gram_arrival(step).wait_recv()

    inverse_factor(gram)

    row = lax.broadcasted_iota(jnp.int32, (ROWS, ROWS), 0)
    col = lax.broadcasted_iota(jnp.int32, (ROWS, ROWS), 1)
    inverse = jnp.where(col <= row, gram[...], F32(0)) * F32(RANK)
    result[...] = exact_dot(inverse, flat, ((1,), (0,))).reshape(SLABS, CHIPS, RANK)

    def back_copy(step):
        to = (z + step) % SLABS
        return pltpu.make_async_remote_copy(
            result.at[to],
            returned.at[z],
            back_send.at[step],
            back_recv.at[z],
            device_id=(to, p),
            device_id_type=MESH,
        )

    def back_arrival(step):
        source = (z + step) % SLABS
        return pltpu.make_async_remote_copy(
            result.at[source],
            returned.at[source],
            back_send.at[step],
            back_recv.at[source],
            device_id=(source, p),
            device_id_type=MESH,
        )

    @pl.loop(1, SLABS)
    def _(step):
        back_copy(step).start()

    out[z] = result[z]

    @pl.loop(1, SLABS)
    def _(step):
        back_arrival(step).wait_recv()
        source = (z + step) % SLABS
        out[source] = returned[source]

    @pl.loop(0, CHIPS - 1)
    def _(step):
        for core in range(CORES):
            piece(step, core).wait_send()

    piece(CHIPS - 1, 1 - h).wait_send()

    @pl.loop(1, COLS)
    def _(step):
        row_copy(step).wait_send()

    @pl.loop(1, SLABS)
    def _(step):
        slice_copy(step).wait_send()
        back_copy(step).wait_send()

    @pl.loop(1, CHIPS)
    def _(step):
        term_copy(step).wait_send()
        block_copy(step).wait_send()
        gram_copy(step).wait_send()


def on_device(tensor, signs3, picked3, signs2, picked2):
    vmem = pl.BlockSpec(memory_space=pltpu.VMEM)
    dma = pltpu.SemaphoreType.DMA
    places = SLABS * CORES
    return pl.pallas_call(
        kernel,
        out_shape=jax.ShapeDtypeStruct((RANK // COLS, CHIPS, RANK), F32),
        in_specs=[pl.BlockSpec(memory_space=pl.ANY)] + [vmem] * 4,
        out_specs=vmem,
        scratch_shapes=[
            pltpu.VMEM((CHIPS, WIDTH, LENGTH), F32),
            pltpu.VMEM((LENGTH, RANK), BF16),
            pltpu.VMEM((CHIPS, RANK, HALF), BF16),
            pltpu.VMEM((CHIPS, CORES, WIDTH, HALF), F32),
            pltpu.VMEM((COLS, WIDTH, HALF), F32),
            pltpu.VMEM((COLS, RANK // COLS, HALF), F32),
            pltpu.VMEM((CHIPS, CORES, RANK // COLS, HALF), F32),
            pltpu.VMEM((SLABS, CHIPS, RANK), F32),
            pltpu.VMEM((SLABS, CHIPS, RANK), F32),
            pltpu.VMEM((CHIPS, BLOCK, ROWS), F32),
            pltpu.VMEM((CHIPS, BLOCK, ROWS), F32),
            pltpu.VMEM((BLOCK, ROWS), F32),
            pltpu.VMEM((places, BLOCK, ROWS), F32),
            pltpu.VMEM((BLOCK, ROWS), F32),
            pltpu.VMEM((ROWS, ROWS), F32),
            pltpu.VMEM((SLABS, CHIPS, RANK), F32),
            pltpu.VMEM((SLABS, CHIPS, RANK), F32),
            dma((CHIPS,)),
            dma((CHIPS, CORES)),
            dma((COLS,)),
            dma((COLS,)),
            dma((COLS,)),
            dma((SLABS,)),
            dma((SLABS,)),
            dma((CHIPS,)),
            dma((CHIPS,)),
            dma((places,)),
            dma((places,)),
            dma((CHIPS,)),
            dma((CHIPS,)),
            dma((SLABS,)),
            dma((SLABS,)),
        ],
        compiler_params=pltpu.CompilerParams(
            collective_id=0, has_side_effects=True, vmem_limit_bytes=40 * 1024 * 1024
        ),
        name="sketch_basis",
    )(
        tensor,
        signs3.reshape(LENGTH // HALF, HALF),
        picked3.reshape(RANK // HALF, HALF),
        signs2.reshape(CHIPS, HALF),
        picked2.reshape(RANK // HALF, HALF),
    )


def solution(mesh):
    placed = (P("slab", "col", None), P(), P(), P(), P())
    return jax.shard_map(
        on_device, mesh=mesh, in_specs=placed, out_specs=P("col", "slab", None), check_vma=False
    )
```

```python
import jax
import jax.numpy as jnp
from jax import lax
from jax.experimental import pallas as pl
from jax.experimental.pallas import tpu as pltpu
from jax.sharding import PartitionSpec as P

MESH = pl.DeviceIdType.MESH
SIDE = 4
CHIPS = SIDE * SIDE
CORES = 2
COLS = CHIPS * CORES
SLABS = 8
WIDTH = 64
LENGTH = 2048
RANK = 256
HALF = 128
ROWS = SLABS * CHIPS
BLOCK = 8
TURNS = sorted(
    ((dx, dy) for dx in range(SIDE) for dy in range(SIDE)),
    key=lambda turn: -sum(min(step, SIDE - step) for step in turn),
)
CHIP_STEPS = TURNS[:-1]
PLANE_STEPS = [(dx, dy, dc) for dx, dy in TURNS for dc in (1, 0)][:-1]
SLAB_STEPS = [4, 3, 5, 2, 6, 1, 7]
PLACE_STEPS = [(dz, dc) for dz in SLAB_STEPS for dc in range(CORES)] + [(0, 1)]
F32 = jnp.float32
BF16 = jnp.bfloat16


def split_two(value):
    high = value.astype(BF16)
    return high, (value - high.astype(F32)).astype(BF16)


def split_three(value):
    high = value.astype(BF16)
    rest = value - high.astype(F32)
    middle = rest.astype(BF16)
    return high, middle, (rest - middle.astype(F32)).astype(BF16)


def exact_dot(left, right, dims):
    lh, lm, ll = split_three(left)
    rh, rm, rl = split_three(right)
    (la,), (ra,) = dims
    return lax.dot_general(
        jnp.concatenate([lh, lh, lm, lm, lh, ll], axis=la),
        jnp.concatenate([rh, rm, rh, rm, rl, rh], axis=ra),
        (dims, ((), ())),
        preferred_element_type=F32,
    )


def odd(value):
    value = value ^ (value >> 8)
    value = value ^ (value >> 4)
    value = value ^ (value >> 2)
    value = value ^ (value >> 1)
    return (1 - 2 * (value & 1)).astype(F32)


def inverse_factor(held):
    lane = lax.broadcasted_iota(jnp.int32, (BLOCK, ROWS), 1)
    sub = lax.broadcasted_iota(jnp.int32, (BLOCK, ROWS), 0)
    for base in range(0, ROWS, BLOCK):
        rows = [
            jnp.broadcast_to(held[base + i : base + i + 1, :], (BLOCK, ROWS)) for i in range(BLOCK)
        ]
        cell = {}
        for i in range(BLOCK):
            for j in range(i + 1):
                cell[i, j] = jnp.broadcast_to(rows[i][:, base + j : base + j + 1], (BLOCK, ROWS))
        own = jnp.logical_and(lane >= base, lane < base + BLOCK)
        rows = [
            jnp.where(own, jnp.where(lane == base + i, F32(1), F32(0)), rows[i])
            for i in range(BLOCK)
        ]
        for k in range(BLOCK):
            root = lax.rsqrt(cell[k, k])
            rows[k] = rows[k] * root
            for i in range(k + 1, BLOCK):
                cell[i, k] = cell[i, k] * root
            for i in range(k + 1, BLOCK):
                for j in range(k + 1, i + 1):
                    cell[i, j] = cell[i, j] - cell[i, k] * cell[j, k]
                rows[i] = rows[i] - cell[i, k] * rows[k]
        tile = rows[0]
        for i in range(1, BLOCK):
            tile = jnp.where(sub == i, rows[i], tile)
        held[base : base + BLOCK, :] = tile
        if base + BLOCK < ROWS:
            update = exact_dot(tile, tile, ((0,), (0,)))
            rest = held[base + BLOCK :, :]
            clear = lax.broadcasted_iota(jnp.int32, rest.shape, 1)
            clear = jnp.logical_and(clear >= base, clear < base + BLOCK)
            held[base + BLOCK :, :] = jnp.where(clear, F32(0), rest) - update[base + BLOCK :, :]


def kernel(
    tensor, signs3_in, picked3_in, signs2_in, picked2_in, out,
    signs3, picked3, signs2, picked2, slabs, table3, table2, outgoing, landed, sketch, spread, slices, planes,
    partial_gram, terms, row_block, blocks, block, gram, result, returned,
    small_sem, load_sem, send_sem, recv_sem, spread_send, spread_recv, slice_send, slice_recv,
    term_send, term_recv, block_send, block_recv, gram_send, gram_recv, back_send, back_recv,
):
    z = lax.axis_index("slab")
    p = lax.axis_index("col")
    q = p // CORES
    h = p % CORES
    x, y = q // SIDE, q % SIDE

    def chip_at(dx, dy):
        return ((x + dx) & (SIDE - 1)) * SIDE + ((y + dy) & (SIDE - 1))

    def device_at(dx, dy, dc):
        return chip_at(dx, dy) * CORES + (h ^ dc)

    def slab_at(dz):
        return (z + dz) & (SLABS - 1)

    barrier = pltpu.get_barrier_semaphore()
    for step in PLANE_STEPS:
        pl.semaphore_signal(barrier, 1, device_id=(z, device_at(*step)), device_id_type=MESH)
    for dz, dc in PLACE_STEPS[:-1]:
        pl.semaphore_signal(
            barrier, 1, device_id=(slab_at(dz), q * CORES + (h ^ dc)), device_id_type=MESH
        )

    def load(step):
        return pltpu.make_async_copy(tensor.at[chip_at(*TURNS[step])], slabs.at[step], load_sem.at[step])

    small = [
        pltpu.make_async_copy(source, target, small_sem.at[n])
        for n, (source, target) in enumerate(
            [(picked3_in, picked3), (picked2_in, picked2), (signs2_in, signs2), (signs3_in, signs3)]
        )
    ]
    for copy in small:
        copy.start()

    for step in range(CHIPS):
        load(step).start()

    for copy in small:
        copy.wait()

    below = lax.broadcasted_iota(jnp.int32, (HALF, HALF), 0)
    for half in range(RANK // HALF):
        picks = picked3[half : half + 1, :]
        low = odd(below & jnp.broadcast_to(picks, (HALF, HALF)))
        for tile in range(LENGTH // HALF):
            high = odd(jnp.broadcast_to(picks, (BLOCK, HALF)) & (tile * HALF))[:1]
            table3[tile * HALF : (tile + 1) * HALF, half * HALF : (half + 1) * HALF] = (
                low * high
            ).astype(BF16)
    along = lax.broadcasted_iota(jnp.int32, (HALF, HALF), 1)
    for half in range(RANK // HALF):
        picks = picked2[half : half + 1, :].astype(F32)
        picks = jnp.broadcast_to(picks, (HALF, HALF)).T.astype(jnp.int32)
        low = odd(along & picks)
        for tile in range(CHIPS):
            high = odd(picks & (tile * HALF))
            signs = signs2[tile : tile + 1, :].astype(F32)
            table2[tile, half * HALF : (half + 1) * HALF, :] = (low * high * signs).astype(BF16)

    def piece(step, core):
        return pltpu.make_async_remote_copy(
            outgoing.at[step, core],
            landed.at[p],
            send_sem.at[step, core],
            recv_sem.at[p],
            device_id=(z, chip_at(*TURNS[step]) * CORES + core),
            device_id_type=MESH,
        )

    for step in range(0, CHIPS, 2):
        load(step).wait()
        load(step + 1).wait()
        both = slabs[step : step + 2].reshape(2 * WIDTH, LENGTH)
        highs, lows = [], []
        for tile in range(LENGTH // HALF):
            signs = signs3[tile : tile + 1, :].astype(F32)
            high, low = split_two(both[:, tile * HALF : (tile + 1) * HALF] * signs)
            highs.append(high)
            lows.append(low)
        left = jnp.concatenate(
            [jnp.concatenate(highs, axis=1), jnp.concatenate(lows, axis=1)], axis=0
        )
        first = jnp.dot(left, table3[...], preferred_element_type=F32)
        first = first[: 2 * WIDTH] + first[2 * WIDTH :]
        for part in range(2):
            for core in range(CORES):
                outgoing[step + part, core] = first[
                    part * WIDTH : (part + 1) * WIDTH, core * HALF : (core + 1) * HALF
                ]
        if step == 0:
            pl.semaphore_wait(barrier, len(PLANE_STEPS) + len(PLACE_STEPS) - 1)
        for part in range(2):
            if step + part < CHIPS - 1:
                for core in range(CORES):
                    piece(step + part, core).start()
            else:
                piece(step + part, 1 - h).start()

    landed[p] = outgoing[CHIPS - 1, h]

    def arrival(source):
        return pltpu.make_async_remote_copy(
            outgoing.at[0, 0],
            landed.at[source],
            send_sem.at[0, 0],
            recv_sem.at[source],
            device_id=(z, p ^ 1),
            device_id_type=MESH,
        )

    total = jnp.zeros((RANK, 2 * HALF), F32)
    for step in range(0, CHIPS, 2):
        lefts, rights = [], []
        for dx, dy in TURNS[step : step + 2]:
            chip = chip_at(-dx, -dy)
            if dx or dy:
                for core in range(CORES):
                    arrival(chip * CORES + core).wait_recv()
            else:
                arrival(p ^ 1).wait_recv()
            lefts.append(table2[chip])
            value = landed[pl.ds(chip * CORES, CORES)].reshape(CORES * WIDTH, HALF)
            rights.append(jnp.concatenate(split_two(value), axis=1))
        total = total + jnp.dot(
            jnp.concatenate(lefts, axis=1),
            jnp.concatenate(rights, axis=0),
            preferred_element_type=F32,
        )
    sketch[...] = (total[:, :HALF] + total[:, HALF:]).reshape(COLS, RANK // COLS, HALF)

    def row_copy(step):
        to = device_at(*PLANE_STEPS[step])
        return pltpu.make_async_remote_copy(
            sketch.at[to],
            spread.at[q, h],
            spread_send.at[step],
            spread_recv.at[p],
            device_id=(z, to),
            device_id_type=MESH,
        )

    def row_arrival(step):
        source = device_at(*PLANE_STEPS[step])
        return pltpu.make_async_remote_copy(
            sketch.at[source],
            spread.at[source // CORES, source % CORES],
            spread_send.at[step],
            spread_recv.at[source],
            device_id=(z, source),
            device_id_type=MESH,
        )

    for step in range(len(PLANE_STEPS)):
        row_copy(step).start()

    spread[q, h] = sketch[p]

    for step in range(len(PLANE_STEPS)):
        row_arrival(step).wait_recv()

    for core in range(CORES):
        for r in range(SLABS):
            slices[r, :, core * HALF : (core + 1) * HALF] = spread[:, core, r, :]

    def slice_copy(step):
        to = slab_at(SLAB_STEPS[step])
        return pltpu.make_async_remote_copy(
            slices.at[to],
            planes.at[z],
            slice_send.at[step],
            slice_recv.at[z],
            device_id=(to, p),
            device_id_type=MESH,
        )

    def slice_arrival(step):
        source = slab_at(SLAB_STEPS[step])
        return pltpu.make_async_remote_copy(
            slices.at[source],
            planes.at[source],
            slice_send.at[step],
            slice_recv.at[source],
            device_id=(source, p),
            device_id_type=MESH,
        )

    for step in range(len(SLAB_STEPS)):
        slice_copy(step).start()

    planes[z] = slices[z]

    for step in range(len(SLAB_STEPS)):
        slice_arrival(step).wait_recv()

    flat = planes[...].reshape(ROWS, RANK)
    partial_gram[...] = exact_dot(flat, flat, ((1,), (1,))).reshape(CHIPS, BLOCK, ROWS)

    def term_copy(step):
        to = chip_at(*CHIP_STEPS[step])
        return pltpu.make_async_remote_copy(
            partial_gram.at[to],
            terms.at[q],
            term_send.at[step],
            term_recv.at[q],
            device_id=(z, to * CORES + h),
            device_id_type=MESH,
        )

    def term_arrival(step):
        source = chip_at(*CHIP_STEPS[step])
        return pltpu.make_async_remote_copy(
            partial_gram.at[source],
            terms.at[source],
            term_send.at[step],
            term_recv.at[source],
            device_id=(z, source * CORES + h),
            device_id_type=MESH,
        )

    for step in range(len(CHIP_STEPS)):
        term_copy(step).start()

    terms[q] = partial_gram[q]

    for step in range(len(CHIP_STEPS)):
        term_arrival(step).wait_recv()

    row_block[...] = jnp.sum(terms[...], axis=0)

    place = z * CORES + h

    def block_copy(step):
        dz, dc = PLACE_STEPS[step]
        return pltpu.make_async_remote_copy(
            row_block,
            blocks.at[place],
            block_send.at[step],
            block_recv.at[place],
            device_id=(slab_at(dz), q * CORES + (h ^ dc)),
            device_id_type=MESH,
        )

    def block_arrival(step):
        dz, dc = PLACE_STEPS[step]
        source = slab_at(dz) * CORES + (h ^ dc)
        return pltpu.make_async_remote_copy(
            row_block,
            blocks.at[source],
            block_send.at[step],
            block_recv.at[source],
            device_id=(slab_at(dz), q * CORES + (h ^ dc)),
            device_id_type=MESH,
        )

    for step in range(len(PLACE_STEPS)):
        block_copy(step).start()

    blocks[place] = row_block[...]

    for step in range(len(PLACE_STEPS)):
        block_arrival(step).wait_recv()

    block[...] = jnp.sum(blocks[...], axis=0)

    def gram_copy(step):
        to = chip_at(*CHIP_STEPS[step])
        return pltpu.make_async_remote_copy(
            block,
            gram.at[pl.ds(q * BLOCK, BLOCK)],
            gram_send.at[step],
            gram_recv.at[q],
            device_id=(z, to * CORES + h),
            device_id_type=MESH,
        )

    def gram_arrival(step):
        source = chip_at(*CHIP_STEPS[step])
        return pltpu.make_async_remote_copy(
            block,
            gram.at[pl.ds(source * BLOCK, BLOCK)],
            gram_send.at[step],
            gram_recv.at[source],
            device_id=(z, source * CORES + h),
            device_id_type=MESH,
        )

    for step in range(len(CHIP_STEPS)):
        gram_copy(step).start()

    gram[pl.ds(pl.multiple_of(q * BLOCK, BLOCK), BLOCK), :] = block[...]

    for step in range(len(CHIP_STEPS)):
        gram_arrival(step).wait_recv()

    inverse_factor(gram)

    row = lax.broadcasted_iota(jnp.int32, (ROWS, ROWS), 0)
    col = lax.broadcasted_iota(jnp.int32, (ROWS, ROWS), 1)
    inverse = jnp.where(col <= row, gram[...], F32(0)) * F32(RANK)
    result[...] = exact_dot(inverse, flat, ((1,), (0,))).reshape(SLABS, CHIPS, RANK)

    def back_copy(step):
        to = slab_at(SLAB_STEPS[step])
        return pltpu.make_async_remote_copy(
            result.at[to],
            returned.at[z],
            back_send.at[step],
            back_recv.at[z],
            device_id=(to, p),
            device_id_type=MESH,
        )

    def back_arrival(step):
        source = slab_at(SLAB_STEPS[step])
        return pltpu.make_async_remote_copy(
            result.at[source],
            returned.at[source],
            back_send.at[step],
            back_recv.at[source],
            device_id=(source, p),
            device_id_type=MESH,
        )

    for step in range(len(SLAB_STEPS)):
        back_copy(step).start()

    out[z] = result[z]

    for step in range(len(SLAB_STEPS)):
        back_arrival(step).wait_recv()
        source = slab_at(SLAB_STEPS[step])
        out[source] = returned[source]

    for step in range(CHIPS - 1):
        for core in range(CORES):
            piece(step, core).wait_send()

    piece(CHIPS - 1, 1 - h).wait_send()

    for step in range(len(PLANE_STEPS)):
        row_copy(step).wait_send()

    for step in range(len(SLAB_STEPS)):
        slice_copy(step).wait_send()
        back_copy(step).wait_send()

    for step in range(len(CHIP_STEPS)):
        term_copy(step).wait_send()
        block_copy(step).wait_send()
        gram_copy(step).wait_send()


def on_device(tensor, signs3, picked3, signs2, picked2):
    vmem = pl.BlockSpec(memory_space=pltpu.VMEM)
    dma = pltpu.SemaphoreType.DMA
    places = SLABS * CORES
    return pl.pallas_call(
        kernel,
        out_shape=jax.ShapeDtypeStruct((RANK // COLS, CHIPS, RANK), F32),
        in_specs=[pl.BlockSpec(memory_space=pl.ANY)] * 5,
        out_specs=vmem,
        scratch_shapes=[
            pltpu.VMEM((LENGTH // HALF, HALF), jnp.int32),
            pltpu.VMEM((RANK // HALF, HALF), jnp.int32),
            pltpu.VMEM((CHIPS, HALF), jnp.int32),
            pltpu.VMEM((RANK // HALF, HALF), jnp.int32),
            pltpu.VMEM((CHIPS, WIDTH, LENGTH), F32),
            pltpu.VMEM((LENGTH, RANK), BF16),
            pltpu.VMEM((CHIPS, RANK, HALF), BF16),
            pltpu.VMEM((CHIPS, CORES, WIDTH, HALF), F32),
            pltpu.VMEM((COLS, WIDTH, HALF), F32),
            pltpu.VMEM((COLS, RANK // COLS, HALF), F32),
            pltpu.VMEM((CHIPS, CORES, RANK // COLS, HALF), F32),
            pltpu.VMEM((SLABS, CHIPS, RANK), F32),
            pltpu.VMEM((SLABS, CHIPS, RANK), F32),
            pltpu.VMEM((CHIPS, BLOCK, ROWS), F32),
            pltpu.VMEM((CHIPS, BLOCK, ROWS), F32),
            pltpu.VMEM((BLOCK, ROWS), F32),
            pltpu.VMEM((places, BLOCK, ROWS), F32),
            pltpu.VMEM((BLOCK, ROWS), F32),
            pltpu.VMEM((ROWS, ROWS), F32),
            pltpu.VMEM((SLABS, CHIPS, RANK), F32),
            pltpu.VMEM((SLABS, CHIPS, RANK), F32),
            dma((4,)),
            dma((CHIPS,)),
            dma((CHIPS, CORES)),
            dma((COLS,)),
            dma((COLS,)),
            dma((COLS,)),
            dma((SLABS,)),
            dma((SLABS,)),
            dma((CHIPS,)),
            dma((CHIPS,)),
            dma((places,)),
            dma((places,)),
            dma((CHIPS,)),
            dma((CHIPS,)),
            dma((SLABS,)),
            dma((SLABS,)),
        ],
        compiler_params=pltpu.CompilerParams(
            collective_id=0, has_side_effects=True, vmem_limit_bytes=64 * 1024 * 1024
        ),
        name="sketch_basis",
    )(
        tensor,
        signs3.reshape(LENGTH // HALF, HALF),
        picked3.reshape(RANK // HALF, HALF),
        signs2.reshape(CHIPS, HALF),
        picked2.reshape(RANK // HALF, HALF),
    )


def solution(mesh):
    placed = (P("slab", "col", None), P(), P(), P(), P())
    return jax.shard_map(
        on_device, mesh=mesh, in_specs=placed, out_specs=P("col", "slab", None), check_vma=False
    )
```

```python
import jax
import jax.numpy as jnp
from jax import lax
from jax.experimental import pallas as pl
from jax.experimental.pallas import tpu as pltpu
from jax.sharding import PartitionSpec as P

MESH = pl.DeviceIdType.MESH
SIDE = 4
CHIPS = SIDE * SIDE
CORES = 2
COLS = CHIPS * CORES
SLABS = 8
WIDTH = 64
LENGTH = 2048
RANK = 256
HALF = 128
ROWS = SLABS * CHIPS
BLOCK = 8
TURNS = sorted(
    ((dx, dy) for dx in range(SIDE) for dy in range(SIDE)),
    key=lambda turn: -sum(min(step, SIDE - step) for step in turn),
)
CHIP_STEPS = TURNS[:-1]
PLANE_STEPS = [(dx, dy, dc) for dx, dy in TURNS for dc in (1, 0)][:-1]
SLAB_STEPS = [4, 3, 5, 2, 6, 1, 7]
PLACE_STEPS = [(dz, dc) for dz in SLAB_STEPS for dc in range(CORES)] + [(0, 1)]
PAIRS = CHIPS // 2
CHUNKS = 2
GROUP = PAIRS // CHUNKS
LOADS = [n + PAIRS * part for n in range(PAIRS) for part in range(2)]
F32 = jnp.float32
BF16 = jnp.bfloat16


def split_two(value):
    high = value.astype(BF16)
    return high, (value - high.astype(F32)).astype(BF16)


def split_three(value):
    high = value.astype(BF16)
    rest = value - high.astype(F32)
    middle = rest.astype(BF16)
    return high, middle, (rest - middle.astype(F32)).astype(BF16)


def exact_dot(left, right, dims):
    lh, lm, ll = split_three(left)
    rh, rm, rl = split_three(right)
    (la,), (ra,) = dims
    return lax.dot_general(
        jnp.concatenate([lh, lh, lm, lm, lh, ll], axis=la),
        jnp.concatenate([rh, rm, rh, rm, rl, rh], axis=ra),
        (dims, ((), ())),
        preferred_element_type=F32,
    )


def odd(value):
    value = value ^ (value >> 8)
    value = value ^ (value >> 4)
    value = value ^ (value >> 2)
    value = value ^ (value >> 1)
    return (1 - 2 * (value & 1)).astype(F32)


def inverse_factor(held):
    lane = lax.broadcasted_iota(jnp.int32, (BLOCK, ROWS), 1)
    sub = lax.broadcasted_iota(jnp.int32, (BLOCK, ROWS), 0)
    for base in range(0, ROWS, BLOCK):
        rows = [
            jnp.broadcast_to(held[base + i : base + i + 1, :], (BLOCK, ROWS)) for i in range(BLOCK)
        ]
        cell = {}
        for i in range(BLOCK):
            for j in range(i + 1):
                cell[i, j] = jnp.broadcast_to(rows[i][:, base + j : base + j + 1], (BLOCK, ROWS))
        own = jnp.logical_and(lane >= base, lane < base + BLOCK)
        rows = [
            jnp.where(own, jnp.where(lane == base + i, F32(1), F32(0)), rows[i])
            for i in range(BLOCK)
        ]
        for k in range(BLOCK):
            root = lax.rsqrt(cell[k, k])
            rows[k] = rows[k] * root
            for i in range(k + 1, BLOCK):
                cell[i, k] = cell[i, k] * root
            for i in range(k + 1, BLOCK):
                for j in range(k + 1, i + 1):
                    cell[i, j] = cell[i, j] - cell[i, k] * cell[j, k]
                rows[i] = rows[i] - cell[i, k] * rows[k]
        tile = rows[0]
        for i in range(1, BLOCK):
            tile = jnp.where(sub == i, rows[i], tile)
        held[base : base + BLOCK, :] = tile
        if base + BLOCK < ROWS:
            update = exact_dot(tile, tile, ((0,), (0,)))
            rest = held[base + BLOCK :, :]
            clear = lax.broadcasted_iota(jnp.int32, rest.shape, 1)
            clear = jnp.logical_and(clear >= base, clear < base + BLOCK)
            held[base + BLOCK :, :] = jnp.where(clear, F32(0), rest) - update[base + BLOCK :, :]


def kernel(
    tensor, signs3_in, picked3_in, signs2_in, picked2_in, out,
    signs3, picked3, signs2, picked2, slabs, table3, table2, outgoing, landed, sketch, slices, planes,
    columns, spread, row_slices, row_planes, partial_gram, terms, row_block, blocks, block, gram, result,
    small_sem, load_sem, send_sem, recv_sem, slice_send, slice_recv, spread_send, spread_recv, row_send, row_recv,
    term_send, term_recv, block_send, block_recv, gram_send, gram_recv, back_send, back_recv,
):
    z = lax.axis_index("slab")
    p = lax.axis_index("col")
    q = p // CORES
    h = p % CORES
    x, y = q // SIDE, q % SIDE

    def chip_at(dx, dy):
        return ((x + dx) & (SIDE - 1)) * SIDE + ((y + dy) & (SIDE - 1))

    def device_at(dx, dy, dc):
        return chip_at(dx, dy) * CORES + (h ^ dc)

    def slab_at(dz):
        return (z + dz) & (SLABS - 1)

    barrier = pltpu.get_barrier_semaphore()
    for step in PLANE_STEPS:
        pl.semaphore_signal(barrier, 1, device_id=(z, device_at(*step)), device_id_type=MESH)
    for dz, dc in PLACE_STEPS[:-1]:
        pl.semaphore_signal(
            barrier, 1, device_id=(slab_at(dz), q * CORES + (h ^ dc)), device_id_type=MESH
        )

    def load(step):
        return pltpu.make_async_copy(tensor.at[step], slabs.at[step], load_sem.at[step])

    small = [
        pltpu.make_async_copy(source, target, small_sem.at[n])
        for n, (source, target) in enumerate(
            [(picked3_in, picked3), (picked2_in, picked2), (signs2_in, signs2), (signs3_in, signs3)]
        )
    ]
    for copy in small:
        copy.start()

    for step in LOADS:
        load(step).start()

    for copy in small:
        copy.wait()

    below = lax.broadcasted_iota(jnp.int32, (HALF, HALF), 0)
    for half in range(RANK // HALF):
        picks = picked3[half : half + 1, :]
        low = odd(below & jnp.broadcast_to(picks, (HALF, HALF)))
        for tile in range(LENGTH // HALF):
            high = odd(jnp.broadcast_to(picks, (BLOCK, HALF)) & (tile * HALF))[:1]
            table3[tile * HALF : (tile + 1) * HALF, half * HALF : (half + 1) * HALF] = (
                low * high
            ).astype(BF16)
    for half in range(RANK // HALF):
        picks = picked2[half : half + 1, :]
        low = odd(below & jnp.broadcast_to(picks, (HALF, HALF)))
        for tile in range(CHIPS):
            high = odd(jnp.broadcast_to(picks, (BLOCK, HALF)) & (tile * HALF))[:1]
            table2[tile, :, half * HALF : (half + 1) * HALF] = (low * high).astype(BF16)

    def piece(chunk, step):
        to = device_at(*PLANE_STEPS[step])
        part = pl.ds(chunk * GROUP, GROUP)
        return pltpu.make_async_remote_copy(
            outgoing.at[to, part],
            landed.at[p, part],
            send_sem.at[chunk, step],
            recv_sem.at[chunk, p],
            device_id=(z, to),
            device_id_type=MESH,
        )

    for chunk in range(CHUNKS):
        start = chunk * GROUP
        for step in LOADS[2 * start : 2 * (start + GROUP)]:
            load(step).wait()
        both = jnp.concatenate(
            [slabs[start : start + GROUP], slabs[PAIRS + start : PAIRS + start + GROUP]], axis=0
        ).reshape(GROUP * HALF, LENGTH)
        highs, lows = [], []
        for tile in range(LENGTH // HALF):
            signs = signs3[tile : tile + 1, :].astype(F32)
            high, low = split_two(both[:, tile * HALF : (tile + 1) * HALF] * signs)
            highs.append(high)
            lows.append(low)
        left = jnp.concatenate(
            [jnp.concatenate(highs, axis=1), jnp.concatenate(lows, axis=1)], axis=0
        )
        first = jnp.dot(left, table3[...], preferred_element_type=F32)
        first = first[: GROUP * HALF] + first[GROUP * HALF :]
        first = first.reshape(2, GROUP, WIDTH, RANK)
        for pair in range(GROUP):
            for half in range(CORES):
                turned = first[:, pair, :, half * HALF : (half + 1) * HALF].reshape(HALF, HALF).T
                outgoing[half * CHIPS : (half + 1) * CHIPS, start + pair] = turned.reshape(
                    CHIPS, BLOCK, HALF
                )
        if chunk == 0:
            pl.semaphore_wait(barrier, len(PLANE_STEPS) + len(PLACE_STEPS) - 1)
        for step in range(len(PLANE_STEPS)):
            piece(chunk, step).start()

    landed[p] = outgoing[p]

    def arrival(source):
        for chunk in range(CHUNKS):
            part = pl.ds(chunk * GROUP, GROUP)
            pltpu.make_async_remote_copy(
                outgoing.at[source, part],
                landed.at[source, part],
                send_sem.at[chunk, 0],
                recv_sem.at[chunk, source],
                device_id=(z, p ^ 1),
                device_id_type=MESH,
            ).wait_recv()

    lane = lax.broadcasted_iota(jnp.int32, (WIDTH, HALF), 1)
    total = jnp.zeros((2 * HALF, RANK), F32)
    for step in range(0, CHIPS, 2):
        lefts, rights = [], []
        for dx, dy in TURNS[step : step + 2]:
            chip = chip_at(-dx, -dy)
            if dx or dy:
                for core in range(CORES):
                    arrival(chip * CORES + core)
            else:
                arrival(p ^ 1)
            even = landed[chip * CORES].reshape(WIDTH, HALF)
            odds = landed[chip * CORES + 1].reshape(WIDTH, HALF)
            value = jnp.concatenate(
                [
                    jnp.where(lane < WIDTH, even, pltpu.roll(odds, WIDTH, 1)),
                    jnp.where(lane < WIDTH, pltpu.roll(even, WIDTH, 1), odds),
                ],
                axis=0,
            )
            value = value * signs2[pl.ds(chip, 1), :].astype(F32)
            lefts.append(jnp.concatenate(split_two(value), axis=0))
            rights.append(table2[chip])
        total = total + jnp.dot(
            jnp.concatenate(lefts, axis=1),
            jnp.concatenate(rights, axis=0),
            preferred_element_type=F32,
        )
    sketch[...] = (total[:HALF] + total[HALF:]).reshape(2, PAIRS, BLOCK, RANK)
    for column in range(BLOCK):
        for part in range(2):
            slices[column, part * PAIRS : (part + 1) * PAIRS, :] = sketch[part, :, column, :]

    def slice_copy(step):
        to = slab_at(SLAB_STEPS[step])
        return pltpu.make_async_remote_copy(
            slices.at[to],
            planes.at[z],
            slice_send.at[step],
            slice_recv.at[z],
            device_id=(to, p),
            device_id_type=MESH,
        )

    def slice_arrival(step):
        source = slab_at(SLAB_STEPS[step])
        return pltpu.make_async_remote_copy(
            slices.at[source],
            planes.at[source],
            slice_send.at[step],
            slice_recv.at[source],
            device_id=(source, p),
            device_id_type=MESH,
        )

    for step in range(len(SLAB_STEPS)):
        slice_copy(step).start()

    planes[z] = slices[z]

    for step in range(len(SLAB_STEPS)):
        slice_arrival(step).wait_recv()

    flat = planes[...].reshape(ROWS, RANK)
    partial_gram[...] = exact_dot(flat, flat, ((1,), (1,))).reshape(CHIPS, BLOCK, ROWS)

    def term_copy(step):
        to = chip_at(*CHIP_STEPS[step])
        return pltpu.make_async_remote_copy(
            partial_gram.at[to],
            terms.at[q],
            term_send.at[step],
            term_recv.at[q],
            device_id=(z, to * CORES + h),
            device_id_type=MESH,
        )

    def term_arrival(step):
        source = chip_at(*CHIP_STEPS[step])
        return pltpu.make_async_remote_copy(
            partial_gram.at[source],
            terms.at[source],
            term_send.at[step],
            term_recv.at[source],
            device_id=(z, source * CORES + h),
            device_id_type=MESH,
        )

    for step in range(len(CHIP_STEPS)):
        term_copy(step).start()

    terms[q] = partial_gram[q]

    across = slices[...].reshape(HALF, RANK)
    for half in range(CORES):
        turned = across[:, half * HALF : (half + 1) * HALF].T
        columns[half * CHIPS : (half + 1) * CHIPS] = turned.reshape(CHIPS, BLOCK, HALF)

    def row_copy(step):
        to = device_at(*PLANE_STEPS[step])
        return pltpu.make_async_remote_copy(
            columns.at[to],
            spread.at[p],
            spread_send.at[step],
            spread_recv.at[p],
            device_id=(z, to),
            device_id_type=MESH,
        )

    def row_arrival(step):
        source = device_at(*PLANE_STEPS[step])
        return pltpu.make_async_remote_copy(
            columns.at[source],
            spread.at[source],
            spread_send.at[step],
            spread_recv.at[source],
            device_id=(z, source),
            device_id_type=MESH,
        )

    for step in range(len(PLANE_STEPS)):
        row_copy(step).start()

    spread[p] = columns[p]

    for step in range(len(CHIP_STEPS)):
        term_arrival(step).wait_recv()

    row_block[...] = jnp.sum(terms[...], axis=0)

    place = z * CORES + h

    def block_copy(step):
        dz, dc = PLACE_STEPS[step]
        return pltpu.make_async_remote_copy(
            row_block,
            blocks.at[place],
            block_send.at[step],
            block_recv.at[place],
            device_id=(slab_at(dz), q * CORES + (h ^ dc)),
            device_id_type=MESH,
        )

    def block_arrival(step):
        dz, dc = PLACE_STEPS[step]
        source = slab_at(dz) * CORES + (h ^ dc)
        return pltpu.make_async_remote_copy(
            row_block,
            blocks.at[source],
            block_send.at[step],
            block_recv.at[source],
            device_id=(slab_at(dz), q * CORES + (h ^ dc)),
            device_id_type=MESH,
        )

    for step in range(len(PLACE_STEPS)):
        block_copy(step).start()

    blocks[place] = row_block[...]

    for step in range(len(PLANE_STEPS)):
        row_arrival(step).wait_recv()
    source_row = lax.broadcasted_iota(jnp.int32, (COLS, RANK), 0)
    source_lane = lax.broadcasted_iota(jnp.int32, (COLS, RANK), 1)
    repeat = jnp.where(source_lane // BLOCK == source_row, F32(1), F32(0)).astype(BF16)
    repeat = jnp.concatenate([repeat] * 3, axis=0)
    kind = lax.broadcasted_iota(jnp.int32, (CHIPS, RANK), 1) % BLOCK
    for r in range(BLOCK):
        thirds = jnp.concatenate(split_three(spread[:, r, :]), axis=0)
        wide = lax.dot_general(
            thirds, repeat, (((0,), (0,)), ((), ())), preferred_element_type=F32
        ).reshape(BLOCK, CHIPS, RANK)
        chosen = wide[0]
        for column in range(1, BLOCK):
            chosen = jnp.where(kind == column, wide[column], chosen)
        row_slices[r] = chosen

    def row_slice_copy(step):
        to = slab_at(SLAB_STEPS[step])
        return pltpu.make_async_remote_copy(
            row_slices.at[to],
            row_planes.at[z],
            row_send.at[step],
            row_recv.at[z],
            device_id=(to, p),
            device_id_type=MESH,
        )

    def row_slice_arrival(step):
        source = slab_at(SLAB_STEPS[step])
        return pltpu.make_async_remote_copy(
            row_slices.at[source],
            row_planes.at[source],
            row_send.at[step],
            row_recv.at[source],
            device_id=(source, p),
            device_id_type=MESH,
        )

    for step in range(len(SLAB_STEPS)):
        row_slice_copy(step).start()

    row_planes[z] = row_slices[z]

    for step in range(len(PLACE_STEPS)):
        block_arrival(step).wait_recv()

    block[...] = jnp.sum(blocks[...], axis=0)

    def gram_copy(step):
        to = chip_at(*CHIP_STEPS[step])
        return pltpu.make_async_remote_copy(
            block,
            gram.at[pl.ds(q * BLOCK, BLOCK)],
            gram_send.at[step],
            gram_recv.at[q],
            device_id=(z, to * CORES + h),
            device_id_type=MESH,
        )

    def gram_arrival(step):
        source = chip_at(*CHIP_STEPS[step])
        return pltpu.make_async_remote_copy(
            block,
            gram.at[pl.ds(source * BLOCK, BLOCK)],
            gram_send.at[step],
            gram_recv.at[source],
            device_id=(z, source * CORES + h),
            device_id_type=MESH,
        )

    for step in range(len(CHIP_STEPS)):
        gram_copy(step).start()

    gram[pl.ds(pl.multiple_of(q * BLOCK, BLOCK), BLOCK), :] = block[...]

    for step in range(len(CHIP_STEPS)):
        gram_arrival(step).wait_recv()

    inverse_factor(gram)

    row = lax.broadcasted_iota(jnp.int32, (ROWS, ROWS), 0)
    col = lax.broadcasted_iota(jnp.int32, (ROWS, ROWS), 1)
    inverse = jnp.where(col <= row, gram[...], F32(0)) * F32(RANK)
    for step in range(len(SLAB_STEPS)):
        row_slice_arrival(step).wait_recv()
    rows = row_planes[...].reshape(ROWS, RANK)
    result[...] = exact_dot(inverse, rows, ((1,), (0,))).reshape(SLABS, CHIPS, RANK)

    def back_copy(step):
        to = slab_at(SLAB_STEPS[step])
        return pltpu.make_async_remote_copy(
            result.at[to],
            out.at[z],
            back_send.at[step],
            back_recv.at[z],
            device_id=(to, p),
            device_id_type=MESH,
        )

    def back_arrival(step):
        source = slab_at(SLAB_STEPS[step])
        return pltpu.make_async_remote_copy(
            result.at[source],
            out.at[source],
            back_send.at[step],
            back_recv.at[source],
            device_id=(source, p),
            device_id_type=MESH,
        )

    for step in range(len(SLAB_STEPS)):
        back_copy(step).start()

    own = pltpu.make_async_copy(result.at[z], out.at[z], back_send.at[len(SLAB_STEPS)])
    own.start()
    for step in range(len(SLAB_STEPS)):
        back_arrival(step).wait_recv()
    own.wait()

    for step in range(len(PLANE_STEPS)):
        for chunk in range(CHUNKS):
            piece(chunk, step).wait_send()

    for step in range(len(PLANE_STEPS)):
        row_copy(step).wait_send()

    for step in range(len(SLAB_STEPS)):
        slice_copy(step).wait_send()
        row_slice_copy(step).wait_send()
        back_copy(step).wait_send()

    for step in range(len(CHIP_STEPS)):
        term_copy(step).wait_send()
        block_copy(step).wait_send()
        gram_copy(step).wait_send()


def on_device(tensor, signs3, picked3, signs2, picked2):
    dma = pltpu.SemaphoreType.DMA
    places = SLABS * CORES
    return pl.pallas_call(
        kernel,
        out_shape=jax.ShapeDtypeStruct((RANK // COLS, CHIPS, RANK), F32),
        in_specs=[pl.BlockSpec(memory_space=pl.ANY)] * 5,
        out_specs=pl.BlockSpec(memory_space=pl.ANY),
        scratch_shapes=[
            pltpu.VMEM((LENGTH // HALF, HALF), jnp.int32),
            pltpu.VMEM((RANK // HALF, HALF), jnp.int32),
            pltpu.VMEM((CHIPS, HALF), jnp.int32),
            pltpu.VMEM((RANK // HALF, HALF), jnp.int32),
            pltpu.VMEM((CHIPS, WIDTH, LENGTH), F32),
            pltpu.VMEM((LENGTH, RANK), BF16),
            pltpu.VMEM((CHIPS, HALF, RANK), BF16),
            pltpu.VMEM((COLS, PAIRS, BLOCK, HALF), F32),
            pltpu.VMEM((COLS, PAIRS, BLOCK, HALF), F32),
            pltpu.VMEM((2, PAIRS, BLOCK, RANK), F32),
            pltpu.VMEM((SLABS, CHIPS, RANK), F32),
            pltpu.VMEM((SLABS, CHIPS, RANK), F32),
            pltpu.VMEM((COLS, BLOCK, HALF), F32),
            pltpu.VMEM((COLS, BLOCK, HALF), F32),
            pltpu.VMEM((SLABS, CHIPS, RANK), F32),
            pltpu.VMEM((SLABS, CHIPS, RANK), F32),
            pltpu.VMEM((CHIPS, BLOCK, ROWS), F32),
            pltpu.VMEM((CHIPS, BLOCK, ROWS), F32),
            pltpu.VMEM((BLOCK, ROWS), F32),
            pltpu.VMEM((places, BLOCK, ROWS), F32),
            pltpu.VMEM((BLOCK, ROWS), F32),
            pltpu.VMEM((ROWS, ROWS), F32),
            pltpu.VMEM((SLABS, CHIPS, RANK), F32),
            dma((4,)),
            dma((CHIPS,)),
            dma((CHUNKS, COLS)),
            dma((CHUNKS, COLS)),
            dma((SLABS,)),
            dma((SLABS,)),
            dma((COLS,)),
            dma((COLS,)),
            dma((SLABS,)),
            dma((SLABS,)),
            dma((CHIPS,)),
            dma((CHIPS,)),
            dma((places,)),
            dma((places,)),
            dma((CHIPS,)),
            dma((CHIPS,)),
            dma((SLABS,)),
            dma((SLABS,)),
        ],
        compiler_params=pltpu.CompilerParams(
            collective_id=0, has_side_effects=True, vmem_limit_bytes=64 * 1024 * 1024
        ),
        name="sketch_basis",
    )(
        tensor,
        signs3.reshape(LENGTH // HALF, HALF),
        picked3.reshape(RANK // HALF, HALF),
        signs2.reshape(CHIPS, HALF),
        picked2.reshape(RANK // HALF, HALF),
    )


def solution(mesh):
    placed = (P("slab", "col", None), P(), P(), P(), P())
    return jax.shard_map(
        on_device, mesh=mesh, in_specs=placed, out_specs=P("col", "slab", None), check_vma=False
    )
```

```python
import jax
import jax.numpy as jnp
from jax import lax
from jax.experimental import pallas as pl
from jax.experimental.pallas import tpu as pltpu
from jax.sharding import PartitionSpec as P

MESH = pl.DeviceIdType.MESH
SIDE = 4
CHIPS = SIDE * SIDE
CORES = 2
COLS = CHIPS * CORES
SLABS = 8
WIDTH = 64
LENGTH = 2048
RANK = 256
HALF = 128
ROWS = SLABS * CHIPS
BLOCK = 8
TURNS = sorted(
    ((dx, dy) for dx in range(SIDE) for dy in range(SIDE)),
    key=lambda turn: -sum(min(step, SIDE - step) for step in turn),
)
CHIP_STEPS = TURNS[:-1]
PLANE_STEPS = [(dx, dy, dc) for dx, dy in TURNS for dc in (1, 0)][:-1]
SLAB_STEPS = [4, 3, 5, 2, 6, 1, 7]
PLACE_STEPS = [(dz, dc) for dz in SLAB_STEPS for dc in range(CORES)] + [(0, 1)]
PAIRS = CHIPS // 2
CHUNKS = 1
GROUP = PAIRS // CHUNKS
BATCH = 4
LOADS = [n + PAIRS * part for n in range(PAIRS) for part in range(2)]
F32 = jnp.float32
BF16 = jnp.bfloat16


def split_two(value):
    high = value.astype(BF16)
    return high, (value - high.astype(F32)).astype(BF16)


def split_three(value):
    high = value.astype(BF16)
    rest = value - high.astype(F32)
    middle = rest.astype(BF16)
    return high, middle, (rest - middle.astype(F32)).astype(BF16)


def exact_dot(left, right, dims):
    lh, lm, ll = split_three(left)
    rh, rm, rl = split_three(right)
    (la,), (ra,) = dims
    return lax.dot_general(
        jnp.concatenate([lh, lh, lm, lm, lh, ll], axis=la),
        jnp.concatenate([rh, rm, rh, rm, rl, rh], axis=ra),
        (dims, ((), ())),
        preferred_element_type=F32,
    )


def odd(value):
    value = value ^ (value >> 8)
    value = value ^ (value >> 4)
    value = value ^ (value >> 2)
    value = value ^ (value >> 1)
    return (1 - 2 * (value & 1)).astype(F32)


def spread_lane(value, lane):
    return jnp.broadcast_to(value[:, lane : lane + 1], value.shape)


def inverse_factor(held):
    lane = lax.broadcasted_iota(jnp.int32, (BLOCK, ROWS), 1)
    sub = lax.broadcasted_iota(jnp.int32, (BLOCK, ROWS), 0)
    rows = [jnp.broadcast_to(held[i : i + 1, :], (BLOCK, ROWS)) for i in range(BLOCK)]
    for base in range(0, ROWS, BLOCK):
        cell = {}
        for i in range(BLOCK):
            for j in range(i + 1):
                cell[i, j] = spread_lane(rows[i], base + j)
        own = jnp.logical_and(lane >= base, lane < base + BLOCK)
        rows = [
            jnp.where(own, jnp.where(lane == base + i, F32(1), F32(0)), rows[i])
            for i in range(BLOCK)
        ]
        for k in range(BLOCK):
            root = lax.rsqrt(cell[k, k])
            rows[k] = rows[k] * root
            for i in range(k + 1, BLOCK):
                cell[i, k] = cell[i, k] * root
            for i in range(k + 1, BLOCK):
                for j in range(k + 1, i + 1):
                    cell[i, j] = cell[i, j] - cell[i, k] * cell[j, k]
                rows[i] = rows[i] - cell[i, k] * rows[k]
        tile = rows[0]
        for i in range(1, BLOCK):
            tile = jnp.where(sub == i, rows[i], tile)
        held[base : base + BLOCK, :] = tile
        after = base + BLOCK
        if after == ROWS:
            break
        coming = []
        for i in range(BLOCK):
            row = jnp.broadcast_to(held[after + i : after + i + 1, :], (BLOCK, ROWS))
            terms = [spread_lane(rows[k], after + i) * rows[k] for k in range(BLOCK)]
            while len(terms) > 1:
                terms = [terms[n] + terms[n + 1] for n in range(0, len(terms), 2)]
            coming.append(jnp.where(own, F32(0), row) - terms[0])
        rows = coming
        after = after + BLOCK
        if after < ROWS:
            update = exact_dot(tile, tile, ((0,), (0,)))
            rest = held[after:, :]
            clear = lax.broadcasted_iota(jnp.int32, rest.shape, 1)
            clear = jnp.logical_and(clear >= base, clear < base + BLOCK)
            held[after:, :] = jnp.where(clear, F32(0), rest) - update[after:, :]


def kernel(
    tensor, signs3_in, picked3_in, signs2_in, picked2_in, out,
    signs3, picked3, signs2, picked2, slabs, table3, table2, outgoing, landed, sketch, slices, planes,
    columns, spread, row_slices, row_planes, partial_gram, terms, row_block, blocks, block, gram, result,
    small_sem, load_sem, send_sem, recv_sem, slice_send, slice_recv, spread_send, spread_recv, row_send, row_recv,
    term_send, term_recv, block_send, block_recv, gram_send, gram_recv, back_send, back_recv,
):
    z = lax.axis_index("slab")
    p = lax.axis_index("col")
    q = p // CORES
    h = p % CORES
    x, y = q // SIDE, q % SIDE

    def chip_at(dx, dy):
        return ((x + dx) & (SIDE - 1)) * SIDE + ((y + dy) & (SIDE - 1))

    def device_at(dx, dy, dc):
        return chip_at(dx, dy) * CORES + (h ^ dc)

    def slab_at(dz):
        return (z + dz) & (SLABS - 1)

    barrier = pltpu.get_barrier_semaphore()
    for step in PLANE_STEPS:
        pl.semaphore_signal(barrier, 1, device_id=(z, device_at(*step)), device_id_type=MESH)
    for dz, dc in PLACE_STEPS[:-1]:
        pl.semaphore_signal(
            barrier, 1, device_id=(slab_at(dz), q * CORES + (h ^ dc)), device_id_type=MESH
        )

    def load(step):
        return pltpu.make_async_copy(tensor.at[step], slabs.at[step], load_sem.at[step])

    small = [
        pltpu.make_async_copy(source, target, small_sem.at[n])
        for n, (source, target) in enumerate(
            [(picked3_in, picked3), (picked2_in, picked2), (signs2_in, signs2), (signs3_in, signs3)]
        )
    ]
    for copy in small:
        copy.start()

    for step in LOADS:
        load(step).start()

    for copy in small:
        copy.wait()

    below = lax.broadcasted_iota(jnp.int32, (HALF, HALF), 0)
    for half in range(RANK // HALF):
        picks = picked3[half : half + 1, :]
        low = odd(below & jnp.broadcast_to(picks, (HALF, HALF)))
        for tile in range(LENGTH // HALF):
            high = odd(jnp.broadcast_to(picks, (BLOCK, HALF)) & (tile * HALF))[:1]
            table3[tile * HALF : (tile + 1) * HALF, half * HALF : (half + 1) * HALF] = (
                low * high
            ).astype(BF16)
    for half in range(RANK // HALF):
        picks = picked2[half : half + 1, :]
        low = odd(below & jnp.broadcast_to(picks, (HALF, HALF)))
        for tile in range(CHIPS):
            high = odd(jnp.broadcast_to(picks, (BLOCK, HALF)) & (tile * HALF))[:1]
            table2[tile, :, half * HALF : (half + 1) * HALF] = (low * high).astype(BF16)

    def piece(chunk, step):
        to = device_at(*PLANE_STEPS[step])
        part = pl.ds(chunk * GROUP, GROUP)
        return pltpu.make_async_remote_copy(
            outgoing.at[to, part],
            landed.at[p, part],
            send_sem.at[chunk, step],
            recv_sem.at[chunk, p],
            device_id=(z, to),
            device_id_type=MESH,
        )

    left = None
    for start in range(0, PAIRS + BATCH, BATCH):
        if start < PAIRS:
            for step in LOADS[2 * start : 2 * (start + BATCH)]:
                load(step).wait()
        if start > 0:
            first = jnp.dot(left, table3[...], preferred_element_type=F32)
            first = first[: BATCH * HALF] + first[BATCH * HALF :]
            first = first.reshape(2, BATCH, WIDTH, RANK)
            for n in range(BATCH):
                for half in range(CORES):
                    turned = first[:, n, :, half * HALF : (half + 1) * HALF]
                    outgoing[half * CHIPS : (half + 1) * CHIPS, start - BATCH + n] = (
                        turned.reshape(HALF, HALF).T.reshape(CHIPS, BLOCK, HALF)
                    )
        if start < PAIRS:
            both = jnp.concatenate(
                [slabs[start : start + BATCH], slabs[PAIRS + start : PAIRS + start + BATCH]],
                axis=0,
            ).reshape(BATCH * HALF, LENGTH)
            highs, lows = [], []
            for tile in range(LENGTH // HALF):
                signs = signs3[tile : tile + 1, :].astype(F32)
                high, low = split_two(both[:, tile * HALF : (tile + 1) * HALF] * signs)
                highs.append(high)
                lows.append(low)
            left = jnp.concatenate(
                [jnp.concatenate(highs, axis=1), jnp.concatenate(lows, axis=1)], axis=0
            )
        if start > 0 and start % GROUP == 0:
            if start == GROUP:
                pl.semaphore_wait(barrier, len(PLANE_STEPS) + len(PLACE_STEPS) - 1)
            for step in range(len(PLANE_STEPS)):
                piece(start // GROUP - 1, step).start()

    landed[p] = outgoing[p]

    def arrival(source):
        for chunk in range(CHUNKS):
            part = pl.ds(chunk * GROUP, GROUP)
            pltpu.make_async_remote_copy(
                outgoing.at[source, part],
                landed.at[source, part],
                send_sem.at[chunk, 0],
                recv_sem.at[chunk, source],
                device_id=(z, p ^ 1),
                device_id_type=MESH,
            ).wait_recv()

    lane = lax.broadcasted_iota(jnp.int32, (WIDTH, HALF), 1)
    total = jnp.zeros((2 * HALF, RANK), F32)
    for step in range(0, CHIPS, 2):
        lefts, rights = [], []
        for dx, dy in TURNS[step : step + 2]:
            chip = chip_at(-dx, -dy)
            if dx or dy:
                for core in range(CORES):
                    arrival(chip * CORES + core)
            else:
                arrival(p ^ 1)
            even = landed[chip * CORES].reshape(WIDTH, HALF)
            odds = landed[chip * CORES + 1].reshape(WIDTH, HALF)
            value = jnp.concatenate(
                [
                    jnp.where(lane < WIDTH, even, pltpu.roll(odds, WIDTH, 1)),
                    jnp.where(lane < WIDTH, pltpu.roll(even, WIDTH, 1), odds),
                ],
                axis=0,
            )
            value = value * signs2[pl.ds(chip, 1), :].astype(F32)
            lefts.append(jnp.concatenate(split_two(value), axis=0))
            rights.append(table2[chip])
        total = total + jnp.dot(
            jnp.concatenate(lefts, axis=1),
            jnp.concatenate(rights, axis=0),
            preferred_element_type=F32,
        )
    sketch[...] = (total[:HALF] + total[HALF:]).reshape(2, PAIRS, BLOCK, RANK)
    for column in range(BLOCK):
        for part in range(2):
            slices[column, part * PAIRS : (part + 1) * PAIRS, :] = sketch[part, :, column, :]

    def slice_copy(step):
        to = slab_at(SLAB_STEPS[step])
        return pltpu.make_async_remote_copy(
            slices.at[to],
            planes.at[z],
            slice_send.at[step],
            slice_recv.at[z],
            device_id=(to, p),
            device_id_type=MESH,
        )

    def slice_arrival(step):
        source = slab_at(SLAB_STEPS[step])
        return pltpu.make_async_remote_copy(
            slices.at[source],
            planes.at[source],
            slice_send.at[step],
            slice_recv.at[source],
            device_id=(source, p),
            device_id_type=MESH,
        )

    for step in range(len(SLAB_STEPS)):
        slice_copy(step).start()

    planes[z] = slices[z]

    for step in range(len(SLAB_STEPS)):
        slice_arrival(step).wait_recv()

    flat = planes[...].reshape(ROWS, RANK)
    partial_gram[...] = exact_dot(flat, flat, ((1,), (1,))).reshape(CHIPS, BLOCK, ROWS)

    def term_copy(step):
        to = chip_at(*CHIP_STEPS[step])
        return pltpu.make_async_remote_copy(
            partial_gram.at[to],
            terms.at[q],
            term_send.at[step],
            term_recv.at[q],
            device_id=(z, to * CORES + h),
            device_id_type=MESH,
        )

    def term_arrival(step):
        source = chip_at(*CHIP_STEPS[step])
        return pltpu.make_async_remote_copy(
            partial_gram.at[source],
            terms.at[source],
            term_send.at[step],
            term_recv.at[source],
            device_id=(z, source * CORES + h),
            device_id_type=MESH,
        )

    for step in range(len(CHIP_STEPS)):
        term_copy(step).start()

    terms[q] = partial_gram[q]

    across = slices[...].reshape(HALF, RANK)
    for half in range(CORES):
        turned = across[:, half * HALF : (half + 1) * HALF].T
        columns[half * CHIPS : (half + 1) * CHIPS] = turned.reshape(CHIPS, BLOCK, HALF)

    def row_copy(step):
        to = device_at(*PLANE_STEPS[step])
        return pltpu.make_async_remote_copy(
            columns.at[to],
            spread.at[p],
            spread_send.at[step],
            spread_recv.at[p],
            device_id=(z, to),
            device_id_type=MESH,
        )

    def row_arrival(step):
        source = device_at(*PLANE_STEPS[step])
        return pltpu.make_async_remote_copy(
            columns.at[source],
            spread.at[source],
            spread_send.at[step],
            spread_recv.at[source],
            device_id=(z, source),
            device_id_type=MESH,
        )

    for step in range(len(PLANE_STEPS)):
        row_copy(step).start()

    spread[p] = columns[p]

    for step in range(len(CHIP_STEPS)):
        term_arrival(step).wait_recv()

    row_block[...] = jnp.sum(terms[...], axis=0)

    place = z * CORES + h

    def block_copy(step):
        dz, dc = PLACE_STEPS[step]
        return pltpu.make_async_remote_copy(
            row_block,
            blocks.at[place],
            block_send.at[step],
            block_recv.at[place],
            device_id=(slab_at(dz), q * CORES + (h ^ dc)),
            device_id_type=MESH,
        )

    def block_arrival(step):
        dz, dc = PLACE_STEPS[step]
        source = slab_at(dz) * CORES + (h ^ dc)
        return pltpu.make_async_remote_copy(
            row_block,
            blocks.at[source],
            block_send.at[step],
            block_recv.at[source],
            device_id=(slab_at(dz), q * CORES + (h ^ dc)),
            device_id_type=MESH,
        )

    for step in range(len(PLACE_STEPS)):
        block_copy(step).start()

    blocks[place] = row_block[...]

    for step in range(len(PLANE_STEPS)):
        row_arrival(step).wait_recv()
    source_row = lax.broadcasted_iota(jnp.int32, (COLS, RANK), 0)
    source_lane = lax.broadcasted_iota(jnp.int32, (COLS, RANK), 1)
    repeat = jnp.where(source_lane // BLOCK == source_row, F32(1), F32(0)).astype(BF16)
    repeat = jnp.concatenate([repeat] * 3, axis=0)
    kind = lax.broadcasted_iota(jnp.int32, (CHIPS, RANK), 1) % BLOCK
    for r in range(BLOCK):
        thirds = jnp.concatenate(split_three(spread[:, r, :]), axis=0)
        wide = lax.dot_general(
            thirds, repeat, (((0,), (0,)), ((), ())), preferred_element_type=F32
        ).reshape(BLOCK, CHIPS, RANK)
        chosen = wide[0]
        for column in range(1, BLOCK):
            chosen = jnp.where(kind == column, wide[column], chosen)
        row_slices[r] = chosen

    def row_slice_copy(step):
        to = slab_at(SLAB_STEPS[step])
        return pltpu.make_async_remote_copy(
            row_slices.at[to],
            row_planes.at[z],
            row_send.at[step],
            row_recv.at[z],
            device_id=(to, p),
            device_id_type=MESH,
        )

    def row_slice_arrival(step):
        source = slab_at(SLAB_STEPS[step])
        return pltpu.make_async_remote_copy(
            row_slices.at[source],
            row_planes.at[source],
            row_send.at[step],
            row_recv.at[source],
            device_id=(source, p),
            device_id_type=MESH,
        )

    for step in range(len(SLAB_STEPS)):
        row_slice_copy(step).start()

    row_planes[z] = row_slices[z]

    for step in range(len(PLACE_STEPS)):
        block_arrival(step).wait_recv()

    block[...] = jnp.sum(blocks[...], axis=0)

    def gram_copy(step):
        to = chip_at(*CHIP_STEPS[step])
        return pltpu.make_async_remote_copy(
            block,
            gram.at[pl.ds(q * BLOCK, BLOCK)],
            gram_send.at[step],
            gram_recv.at[q],
            device_id=(z, to * CORES + h),
            device_id_type=MESH,
        )

    def gram_arrival(step):
        source = chip_at(*CHIP_STEPS[step])
        return pltpu.make_async_remote_copy(
            block,
            gram.at[pl.ds(source * BLOCK, BLOCK)],
            gram_send.at[step],
            gram_recv.at[source],
            device_id=(z, source * CORES + h),
            device_id_type=MESH,
        )

    for step in range(len(CHIP_STEPS)):
        gram_copy(step).start()

    gram[pl.ds(pl.multiple_of(q * BLOCK, BLOCK), BLOCK), :] = block[...]

    for step in range(len(CHIP_STEPS)):
        gram_arrival(step).wait_recv()

    inverse_factor(gram)

    row = lax.broadcasted_iota(jnp.int32, (ROWS, ROWS), 0)
    col = lax.broadcasted_iota(jnp.int32, (ROWS, ROWS), 1)
    inverse = jnp.where(col <= row, gram[...], F32(0)) * F32(RANK)
    for step in range(len(SLAB_STEPS)):
        row_slice_arrival(step).wait_recv()
    rows = row_planes[...].reshape(ROWS, RANK)
    result[...] = exact_dot(inverse, rows, ((1,), (0,))).reshape(SLABS, CHIPS, RANK)

    def back_copy(step):
        to = slab_at(SLAB_STEPS[step])
        return pltpu.make_async_remote_copy(
            result.at[to],
            out.at[z],
            back_send.at[step],
            back_recv.at[z],
            device_id=(to, p),
            device_id_type=MESH,
        )

    def back_arrival(step):
        source = slab_at(SLAB_STEPS[step])
        return pltpu.make_async_remote_copy(
            result.at[source],
            out.at[source],
            back_send.at[step],
            back_recv.at[source],
            device_id=(source, p),
            device_id_type=MESH,
        )

    for step in range(len(SLAB_STEPS)):
        back_copy(step).start()

    own = pltpu.make_async_copy(result.at[z], out.at[z], back_send.at[len(SLAB_STEPS)])
    own.start()
    for step in range(len(SLAB_STEPS)):
        back_arrival(step).wait_recv()
    own.wait()

    for step in range(len(PLANE_STEPS)):
        for chunk in range(CHUNKS):
            piece(chunk, step).wait_send()

    for step in range(len(PLANE_STEPS)):
        row_copy(step).wait_send()

    for step in range(len(SLAB_STEPS)):
        slice_copy(step).wait_send()
        row_slice_copy(step).wait_send()
        back_copy(step).wait_send()

    for step in range(len(CHIP_STEPS)):
        term_copy(step).wait_send()
        block_copy(step).wait_send()
        gram_copy(step).wait_send()


def on_device(tensor, signs3, picked3, signs2, picked2):
    dma = pltpu.SemaphoreType.DMA
    places = SLABS * CORES
    return pl.pallas_call(
        kernel,
        out_shape=jax.ShapeDtypeStruct((RANK // COLS, CHIPS, RANK), F32),
        in_specs=[pl.BlockSpec(memory_space=pl.ANY)] * 5,
        out_specs=pl.BlockSpec(memory_space=pl.ANY),
        scratch_shapes=[
            pltpu.VMEM((LENGTH // HALF, HALF), jnp.int32),
            pltpu.VMEM((RANK // HALF, HALF), jnp.int32),
            pltpu.VMEM((CHIPS, HALF), jnp.int32),
            pltpu.VMEM((RANK // HALF, HALF), jnp.int32),
            pltpu.VMEM((CHIPS, WIDTH, LENGTH), F32),
            pltpu.VMEM((LENGTH, RANK), BF16),
            pltpu.VMEM((CHIPS, HALF, RANK), BF16),
            pltpu.VMEM((COLS, PAIRS, BLOCK, HALF), F32),
            pltpu.VMEM((COLS, PAIRS, BLOCK, HALF), F32),
            pltpu.VMEM((2, PAIRS, BLOCK, RANK), F32),
            pltpu.VMEM((SLABS, CHIPS, RANK), F32),
            pltpu.VMEM((SLABS, CHIPS, RANK), F32),
            pltpu.VMEM((COLS, BLOCK, HALF), F32),
            pltpu.VMEM((COLS, BLOCK, HALF), F32),
            pltpu.VMEM((SLABS, CHIPS, RANK), F32),
            pltpu.VMEM((SLABS, CHIPS, RANK), F32),
            pltpu.VMEM((CHIPS, BLOCK, ROWS), F32),
            pltpu.VMEM((CHIPS, BLOCK, ROWS), F32),
            pltpu.VMEM((BLOCK, ROWS), F32),
            pltpu.VMEM((places, BLOCK, ROWS), F32),
            pltpu.VMEM((BLOCK, ROWS), F32),
            pltpu.VMEM((ROWS, ROWS), F32),
            pltpu.VMEM((SLABS, CHIPS, RANK), F32),
            dma((4,)),
            dma((CHIPS,)),
            dma((CHUNKS, COLS)),
            dma((CHUNKS, COLS)),
            dma((SLABS,)),
            dma((SLABS,)),
            dma((COLS,)),
            dma((COLS,)),
            dma((SLABS,)),
            dma((SLABS,)),
            dma((CHIPS,)),
            dma((CHIPS,)),
            dma((places,)),
            dma((places,)),
            dma((CHIPS,)),
            dma((CHIPS,)),
            dma((SLABS,)),
            dma((SLABS,)),
        ],
        compiler_params=pltpu.CompilerParams(
            collective_id=0, has_side_effects=True, vmem_limit_bytes=64 * 1024 * 1024
        ),
        name="sketch_basis",
    )(
        tensor,
        signs3.reshape(LENGTH // HALF, HALF),
        picked3.reshape(RANK // HALF, HALF),
        signs2.reshape(CHIPS, HALF),
        picked2.reshape(RANK // HALF, HALF),
    )


def solution(mesh):
    placed = (P("slab", "col", None), P(), P(), P(), P())
    return jax.shard_map(
        on_device, mesh=mesh, in_specs=placed, out_specs=P("col", "slab", None), check_vma=False
    )
```

```python
import jax
import jax.numpy as jnp
from jax import lax
from jax.experimental import pallas as pl
from jax.experimental.pallas import tpu as pltpu
from jax.sharding import PartitionSpec as P

MESH = pl.DeviceIdType.MESH
SIDE = 4
CHIPS = SIDE * SIDE
CORES = 2
COLS = CHIPS * CORES
SLABS = 8
WIDTH = 64
LENGTH = 2048
RANK = 256
HALF = 128
ROWS = SLABS * CHIPS
BLOCK = 8
TURNS = sorted(
    ((dx, dy) for dx in range(SIDE) for dy in range(SIDE)),
    key=lambda turn: -sum(min(step, SIDE - step) for step in turn),
)
CHIP_STEPS = TURNS[:-1]
PLANE_STEPS = [(dx, dy, dc) for dc in (1, 0) for dx, dy in TURNS][:-1]
SLAB_STEPS = [4, 3, 5, 2, 6, 1, 7]
PLACE_STEPS = [(dz, dc) for dz in SLAB_STEPS for dc in range(CORES)] + [(0, 1)]
PAIRS = CHIPS // 2
CHUNKS = 1
GROUP = PAIRS // CHUNKS
BATCH = 8
LOADS = [n + PAIRS * part for n in range(PAIRS) for part in range(2)]
F32 = jnp.float32
BF16 = jnp.bfloat16


def split_two(value):
    high = value.astype(BF16)
    return high, (value - high.astype(F32)).astype(BF16)


def split_three(value):
    high = value.astype(BF16)
    rest = value - high.astype(F32)
    middle = rest.astype(BF16)
    return high, middle, (rest - middle.astype(F32)).astype(BF16)


def exact_dot(left, right, dims):
    lh, lm, ll = split_three(left)
    rh, rm, rl = split_three(right)
    (la,), (ra,) = dims
    return lax.dot_general(
        jnp.concatenate([lh, lh, lm, lm, lh, ll], axis=la),
        jnp.concatenate([rh, rm, rh, rm, rl, rh], axis=ra),
        (dims, ((), ())),
        preferred_element_type=F32,
    )


def odd(value):
    value = value ^ (value >> 8)
    value = value ^ (value >> 4)
    value = value ^ (value >> 2)
    value = value ^ (value >> 1)
    return (1 - 2 * (value & 1)).astype(F32)


def spread_lane(value, lane):
    return jnp.broadcast_to(value[:, lane : lane + 1], value.shape)


def inverse_factor(held):
    lane = lax.broadcasted_iota(jnp.int32, (BLOCK, ROWS), 1)
    sub = lax.broadcasted_iota(jnp.int32, (BLOCK, ROWS), 0)
    rows = [jnp.broadcast_to(held[i : i + 1, :], (BLOCK, ROWS)) for i in range(BLOCK)]
    for base in range(0, ROWS, BLOCK):
        cell = {}
        for i in range(BLOCK):
            for j in range(i + 1):
                cell[i, j] = spread_lane(rows[i], base + j)
        own = jnp.logical_and(lane >= base, lane < base + BLOCK)
        rows = [
            jnp.where(own, jnp.where(lane == base + i, F32(1), F32(0)), rows[i])
            for i in range(BLOCK)
        ]
        for k in range(BLOCK):
            root = lax.rsqrt(cell[k, k])
            rows[k] = rows[k] * root
            for i in range(k + 1, BLOCK):
                cell[i, k] = cell[i, k] * root
            for i in range(k + 1, BLOCK):
                for j in range(k + 1, i + 1):
                    cell[i, j] = cell[i, j] - cell[i, k] * cell[j, k]
                rows[i] = rows[i] - cell[i, k] * rows[k]
        tile = rows[0]
        for i in range(1, BLOCK):
            tile = jnp.where(sub == i, rows[i], tile)
        held[base : base + BLOCK, :] = tile
        after = base + BLOCK
        if after == ROWS:
            break
        coming = []
        for i in range(BLOCK):
            row = jnp.broadcast_to(held[after + i : after + i + 1, :], (BLOCK, ROWS))
            terms = [spread_lane(rows[k], after + i) * rows[k] for k in range(BLOCK)]
            while len(terms) > 1:
                terms = [terms[n] + terms[n + 1] for n in range(0, len(terms), 2)]
            coming.append(jnp.where(own, F32(0), row) - terms[0])
        rows = coming
        after = after + BLOCK
        if after < ROWS:
            update = exact_dot(tile, tile, ((0,), (0,)))
            rest = held[after:, :]
            clear = lax.broadcasted_iota(jnp.int32, rest.shape, 1)
            clear = jnp.logical_and(clear >= base, clear < base + BLOCK)
            held[after:, :] = jnp.where(clear, F32(0), rest) - update[after:, :]


def kernel(
    tensor, signs3_in, picked3_in, signs2_in, picked2_in, out,
    signs3, picked3, signs2, picked2, slabs, table3, table2, outgoing, landed, sketch, slices, planes,
    columns, spread, row_slices, row_planes, partial_gram, terms, row_block, blocks, block, gram, row_parts, result,
    small_sem, load_sem, send_sem, recv_sem, slice_send, slice_recv, spread_send, spread_recv, row_send, row_recv,
    term_send, term_recv, block_send, block_recv, gram_send, gram_recv, back_send, back_recv,
):
    z = lax.axis_index("slab")
    p = lax.axis_index("col")
    q = p // CORES
    h = p % CORES
    x, y = q // SIDE, q % SIDE

    def chip_at(dx, dy):
        return ((x + dx) & (SIDE - 1)) * SIDE + ((y + dy) & (SIDE - 1))

    def device_at(dx, dy, dc):
        return chip_at(dx, dy) * CORES + (h ^ dc)

    def slab_at(dz):
        return (z + dz) & (SLABS - 1)

    barrier = pltpu.get_barrier_semaphore()
    for step in PLANE_STEPS:
        pl.semaphore_signal(barrier, 1, device_id=(z, device_at(*step)), device_id_type=MESH)
    for dz, dc in PLACE_STEPS[:-1]:
        pl.semaphore_signal(
            barrier, 1, device_id=(slab_at(dz), q * CORES + (h ^ dc)), device_id_type=MESH
        )

    def load(step):
        return pltpu.make_async_copy(tensor.at[step], slabs.at[step], load_sem.at[step])

    small = [
        pltpu.make_async_copy(source, target, small_sem.at[n])
        for n, (source, target) in enumerate(
            [(picked3_in, picked3), (picked2_in, picked2), (signs2_in, signs2), (signs3_in, signs3)]
        )
    ]
    for copy in small:
        copy.start()

    for step in LOADS:
        load(step).start()

    for copy in small:
        copy.wait()

    below = lax.broadcasted_iota(jnp.int32, (HALF, HALF), 0)
    for half in range(RANK // HALF):
        picks = picked3[half : half + 1, :]
        low = odd(below & jnp.broadcast_to(picks, (HALF, HALF)))
        for tile in range(LENGTH // HALF):
            high = odd(jnp.broadcast_to(picks, (BLOCK, HALF)) & (tile * HALF))[:1]
            table3[tile * HALF : (tile + 1) * HALF, half * HALF : (half + 1) * HALF] = (
                low * high
            ).astype(BF16)
    for half in range(RANK // HALF):
        picks = picked2[half : half + 1, :]
        low = odd(below & jnp.broadcast_to(picks, (HALF, HALF)))
        for tile in range(CHIPS):
            high = odd(jnp.broadcast_to(picks, (BLOCK, HALF)) & (tile * HALF))[:1]
            table2[tile, :, half * HALF : (half + 1) * HALF] = (low * high).astype(BF16)

    def piece(chunk, step):
        to = device_at(*PLANE_STEPS[step])
        part = pl.ds(chunk * GROUP, GROUP)
        return pltpu.make_async_remote_copy(
            outgoing.at[to, part],
            landed.at[p, part],
            send_sem.at[chunk, step],
            recv_sem.at[chunk, p],
            device_id=(z, to),
            device_id_type=MESH,
        )

    left = None
    for start in range(0, PAIRS + BATCH, BATCH):
        if start < PAIRS:
            for step in LOADS[2 * start : 2 * (start + BATCH)]:
                load(step).wait()
        if start > 0:
            first = jnp.dot(left, table3[...], preferred_element_type=F32)
            first = first[: BATCH * HALF] + first[BATCH * HALF :]
            first = first.reshape(2, BATCH, WIDTH, RANK)
            for n in range(BATCH):
                for half in range(CORES):
                    turned = first[:, n, :, half * HALF : (half + 1) * HALF]
                    outgoing[half * CHIPS : (half + 1) * CHIPS, start - BATCH + n] = (
                        turned.reshape(HALF, HALF).T.reshape(CHIPS, BLOCK, HALF)
                    )
        if start < PAIRS:
            both = jnp.concatenate(
                [slabs[start : start + BATCH], slabs[PAIRS + start : PAIRS + start + BATCH]],
                axis=0,
            ).reshape(BATCH * HALF, LENGTH)
            highs, lows = [], []
            for tile in range(LENGTH // HALF):
                signs = signs3[tile : tile + 1, :].astype(F32)
                high, low = split_two(both[:, tile * HALF : (tile + 1) * HALF] * signs)
                highs.append(high)
                lows.append(low)
            left = jnp.concatenate(
                [jnp.concatenate(highs, axis=1), jnp.concatenate(lows, axis=1)], axis=0
            )
        if start > 0 and start % GROUP == 0:
            if start == GROUP:
                pl.semaphore_wait(barrier, len(PLANE_STEPS) + len(PLACE_STEPS) - 1)
            for step in range(len(PLANE_STEPS)):
                piece(start // GROUP - 1, step).start()

    landed[p] = outgoing[p]

    def arrival(source):
        for chunk in range(CHUNKS):
            part = pl.ds(chunk * GROUP, GROUP)
            pltpu.make_async_remote_copy(
                outgoing.at[source, part],
                landed.at[source, part],
                send_sem.at[chunk, 0],
                recv_sem.at[chunk, source],
                device_id=(z, p ^ 1),
                device_id_type=MESH,
            ).wait_recv()

    lane = lax.broadcasted_iota(jnp.int32, (WIDTH, HALF), 1)
    total = jnp.zeros((2 * HALF, RANK), F32)
    for step in range(0, CHIPS, 2):
        lefts, rights = [], []
        for dx, dy in TURNS[step : step + 2]:
            chip = chip_at(-dx, -dy)
            if dx or dy:
                for core in range(CORES):
                    arrival(chip * CORES + core)
            else:
                arrival(p ^ 1)
            even = landed[chip * CORES].reshape(WIDTH, HALF)
            odds = landed[chip * CORES + 1].reshape(WIDTH, HALF)
            value = jnp.concatenate(
                [
                    jnp.where(lane < WIDTH, even, pltpu.roll(odds, WIDTH, 1)),
                    jnp.where(lane < WIDTH, pltpu.roll(even, WIDTH, 1), odds),
                ],
                axis=0,
            )
            value = value * signs2[pl.ds(chip, 1), :].astype(F32)
            lefts.append(jnp.concatenate(split_two(value), axis=0))
            rights.append(table2[chip])
        total = total + jnp.dot(
            jnp.concatenate(lefts, axis=1),
            jnp.concatenate(rights, axis=0),
            preferred_element_type=F32,
        )
    sketch[...] = (total[:HALF] + total[HALF:]).reshape(2, PAIRS, BLOCK, RANK)
    for column in range(BLOCK):
        for part in range(2):
            slices[column, part * PAIRS : (part + 1) * PAIRS, :] = sketch[part, :, column, :]

    def slice_copy(step):
        to = slab_at(SLAB_STEPS[step])
        return pltpu.make_async_remote_copy(
            slices.at[to],
            planes.at[z],
            slice_send.at[step],
            slice_recv.at[z],
            device_id=(to, p),
            device_id_type=MESH,
        )

    def slice_arrival(step):
        source = slab_at(SLAB_STEPS[step])
        return pltpu.make_async_remote_copy(
            slices.at[source],
            planes.at[source],
            slice_send.at[step],
            slice_recv.at[source],
            device_id=(source, p),
            device_id_type=MESH,
        )

    for step in range(len(SLAB_STEPS)):
        slice_copy(step).start()

    planes[z] = slices[z]

    for step in range(len(SLAB_STEPS)):
        slice_arrival(step).wait_recv()

    flat = planes[...].reshape(ROWS, RANK)
    partial_gram[...] = exact_dot(flat, flat, ((1,), (1,))).reshape(CHIPS, BLOCK, ROWS)

    def term_copy(step):
        to = chip_at(*CHIP_STEPS[step])
        return pltpu.make_async_remote_copy(
            partial_gram.at[to],
            terms.at[q],
            term_send.at[step],
            term_recv.at[q],
            device_id=(z, to * CORES + h),
            device_id_type=MESH,
        )

    def term_arrival(step):
        source = chip_at(*CHIP_STEPS[step])
        return pltpu.make_async_remote_copy(
            partial_gram.at[source],
            terms.at[source],
            term_send.at[step],
            term_recv.at[source],
            device_id=(z, source * CORES + h),
            device_id_type=MESH,
        )

    for step in range(len(CHIP_STEPS)):
        term_copy(step).start()

    terms[q] = partial_gram[q]

    across = slices[...].reshape(HALF, RANK)
    for half in range(CORES):
        turned = across[:, half * HALF : (half + 1) * HALF].T
        columns[half * CHIPS : (half + 1) * CHIPS] = turned.reshape(CHIPS, BLOCK, HALF)

    def row_copy(step):
        to = device_at(*PLANE_STEPS[step])
        return pltpu.make_async_remote_copy(
            columns.at[to],
            spread.at[p],
            spread_send.at[step],
            spread_recv.at[p],
            device_id=(z, to),
            device_id_type=MESH,
        )

    def row_arrival(step):
        source = device_at(*PLANE_STEPS[step])
        return pltpu.make_async_remote_copy(
            columns.at[source],
            spread.at[source],
            spread_send.at[step],
            spread_recv.at[source],
            device_id=(z, source),
            device_id_type=MESH,
        )

    for step in range(len(PLANE_STEPS)):
        row_copy(step).start()

    spread[p] = columns[p]

    for step in range(len(CHIP_STEPS)):
        term_arrival(step).wait_recv()

    row_block[...] = jnp.sum(terms[...], axis=0)

    place = z * CORES + h

    def block_copy(step):
        dz, dc = PLACE_STEPS[step]
        return pltpu.make_async_remote_copy(
            row_block,
            blocks.at[place],
            block_send.at[step],
            block_recv.at[place],
            device_id=(slab_at(dz), q * CORES + (h ^ dc)),
            device_id_type=MESH,
        )

    def block_arrival(step):
        dz, dc = PLACE_STEPS[step]
        source = slab_at(dz) * CORES + (h ^ dc)
        return pltpu.make_async_remote_copy(
            row_block,
            blocks.at[source],
            block_send.at[step],
            block_recv.at[source],
            device_id=(slab_at(dz), q * CORES + (h ^ dc)),
            device_id_type=MESH,
        )

    for step in range(len(PLACE_STEPS)):
        block_copy(step).start()

    blocks[place] = row_block[...]

    for step in range(len(PLANE_STEPS)):
        row_arrival(step).wait_recv()
    source_row = lax.broadcasted_iota(jnp.int32, (COLS, RANK), 0)
    source_lane = lax.broadcasted_iota(jnp.int32, (COLS, RANK), 1)
    repeat = jnp.where(source_lane // BLOCK == source_row, F32(1), F32(0)).astype(BF16)
    repeat = jnp.concatenate([repeat] * 3, axis=0)
    kind = lax.broadcasted_iota(jnp.int32, (CHIPS, RANK), 1) % BLOCK
    for r in range(BLOCK):
        thirds = jnp.concatenate(split_three(spread[:, r, :]), axis=0)
        wide = lax.dot_general(
            thirds, repeat, (((0,), (0,)), ((), ())), preferred_element_type=F32
        ).reshape(BLOCK, CHIPS, RANK)
        chosen = wide[0]
        for column in range(1, BLOCK):
            chosen = jnp.where(kind == column, wide[column], chosen)
        row_slices[r] = chosen

    def row_slice_copy(step):
        to = slab_at(SLAB_STEPS[step])
        return pltpu.make_async_remote_copy(
            row_slices.at[to],
            row_planes.at[z],
            row_send.at[step],
            row_recv.at[z],
            device_id=(to, p),
            device_id_type=MESH,
        )

    def row_slice_arrival(step):
        source = slab_at(SLAB_STEPS[step])
        return pltpu.make_async_remote_copy(
            row_slices.at[source],
            row_planes.at[source],
            row_send.at[step],
            row_recv.at[source],
            device_id=(source, p),
            device_id_type=MESH,
        )

    for step in range(len(SLAB_STEPS)):
        row_slice_copy(step).start()

    row_planes[z] = row_slices[z]

    for step in range(len(PLACE_STEPS)):
        block_arrival(step).wait_recv()

    block[...] = jnp.sum(blocks[...], axis=0)

    def gram_copy(step):
        to = chip_at(*CHIP_STEPS[step])
        return pltpu.make_async_remote_copy(
            block,
            gram.at[pl.ds(q * BLOCK, BLOCK)],
            gram_send.at[step],
            gram_recv.at[q],
            device_id=(z, to * CORES + h),
            device_id_type=MESH,
        )

    def gram_arrival(step):
        source = chip_at(*CHIP_STEPS[step])
        return pltpu.make_async_remote_copy(
            block,
            gram.at[pl.ds(source * BLOCK, BLOCK)],
            gram_send.at[step],
            gram_recv.at[source],
            device_id=(z, source * CORES + h),
            device_id_type=MESH,
        )

    for step in range(len(CHIP_STEPS)):
        gram_copy(step).start()

    gram[pl.ds(pl.multiple_of(q * BLOCK, BLOCK), BLOCK), :] = block[...]

    for step in range(len(SLAB_STEPS)):
        row_slice_arrival(step).wait_recv()
    row_high, row_low = split_two(row_planes[...].reshape(ROWS, RANK))
    row_parts[...] = jnp.concatenate([row_high, row_low, row_high], axis=0)

    for step in range(len(CHIP_STEPS)):
        gram_arrival(step).wait_recv()

    inverse_factor(gram)

    row = lax.broadcasted_iota(jnp.int32, (ROWS, ROWS), 0)
    col = lax.broadcasted_iota(jnp.int32, (ROWS, ROWS), 1)
    inverse = jnp.where(col <= row, gram[...], F32(0)) * F32(RANK)
    high, low = split_two(inverse)
    result[...] = jnp.dot(
        jnp.concatenate([high, high, low], axis=1), row_parts[...], preferred_element_type=F32
    ).reshape(SLABS, CHIPS, RANK)

    def back_copy(step):
        to = slab_at(SLAB_STEPS[step])
        return pltpu.make_async_remote_copy(
            result.at[to],
            out.at[z],
            back_send.at[step],
            back_recv.at[z],
            device_id=(to, p),
            device_id_type=MESH,
        )

    def back_arrival(step):
        source = slab_at(SLAB_STEPS[step])
        return pltpu.make_async_remote_copy(
            result.at[source],
            out.at[source],
            back_send.at[step],
            back_recv.at[source],
            device_id=(source, p),
            device_id_type=MESH,
        )

    for step in range(len(SLAB_STEPS)):
        back_copy(step).start()

    own = pltpu.make_async_copy(result.at[z], out.at[z], back_send.at[len(SLAB_STEPS)])
    own.start()
    for step in range(len(SLAB_STEPS)):
        back_arrival(step).wait_recv()
    own.wait()

    for step in range(len(PLANE_STEPS)):
        for chunk in range(CHUNKS):
            piece(chunk, step).wait_send()

    for step in range(len(PLANE_STEPS)):
        row_copy(step).wait_send()

    for step in range(len(SLAB_STEPS)):
        slice_copy(step).wait_send()
        row_slice_copy(step).wait_send()
        back_copy(step).wait_send()

    for step in range(len(CHIP_STEPS)):
        term_copy(step).wait_send()
        block_copy(step).wait_send()
        gram_copy(step).wait_send()


def on_device(tensor, signs3, picked3, signs2, picked2):
    dma = pltpu.SemaphoreType.DMA
    places = SLABS * CORES
    return pl.pallas_call(
        kernel,
        out_shape=jax.ShapeDtypeStruct((RANK // COLS, CHIPS, RANK), F32),
        in_specs=[pl.BlockSpec(memory_space=pl.ANY)] * 5,
        out_specs=pl.BlockSpec(memory_space=pl.ANY),
        scratch_shapes=[
            pltpu.VMEM((LENGTH // HALF, HALF), jnp.int32),
            pltpu.VMEM((RANK // HALF, HALF), jnp.int32),
            pltpu.VMEM((CHIPS, HALF), jnp.int32),
            pltpu.VMEM((RANK // HALF, HALF), jnp.int32),
            pltpu.VMEM((CHIPS, WIDTH, LENGTH), F32),
            pltpu.VMEM((LENGTH, RANK), BF16),
            pltpu.VMEM((CHIPS, HALF, RANK), BF16),
            pltpu.VMEM((COLS, PAIRS, BLOCK, HALF), F32),
            pltpu.VMEM((COLS, PAIRS, BLOCK, HALF), F32),
            pltpu.VMEM((2, PAIRS, BLOCK, RANK), F32),
            pltpu.VMEM((SLABS, CHIPS, RANK), F32),
            pltpu.VMEM((SLABS, CHIPS, RANK), F32),
            pltpu.VMEM((COLS, BLOCK, HALF), F32),
            pltpu.VMEM((COLS, BLOCK, HALF), F32),
            pltpu.VMEM((SLABS, CHIPS, RANK), F32),
            pltpu.VMEM((SLABS, CHIPS, RANK), F32),
            pltpu.VMEM((CHIPS, BLOCK, ROWS), F32),
            pltpu.VMEM((CHIPS, BLOCK, ROWS), F32),
            pltpu.VMEM((BLOCK, ROWS), F32),
            pltpu.VMEM((places, BLOCK, ROWS), F32),
            pltpu.VMEM((BLOCK, ROWS), F32),
            pltpu.VMEM((ROWS, ROWS), F32),
            pltpu.VMEM((3 * ROWS, RANK), BF16),
            pltpu.VMEM((SLABS, CHIPS, RANK), F32),
            dma((4,)),
            dma((CHIPS,)),
            dma((CHUNKS, COLS)),
            dma((CHUNKS, COLS)),
            dma((SLABS,)),
            dma((SLABS,)),
            dma((COLS,)),
            dma((COLS,)),
            dma((SLABS,)),
            dma((SLABS,)),
            dma((CHIPS,)),
            dma((CHIPS,)),
            dma((places,)),
            dma((places,)),
            dma((CHIPS,)),
            dma((CHIPS,)),
            dma((SLABS,)),
            dma((SLABS,)),
        ],
        compiler_params=pltpu.CompilerParams(
            collective_id=0, has_side_effects=True, vmem_limit_bytes=64 * 1024 * 1024
        ),
        name="sketch_basis",
    )(
        tensor,
        signs3.reshape(LENGTH // HALF, HALF),
        picked3.reshape(RANK // HALF, HALF),
        signs2.reshape(CHIPS, HALF),
        picked2.reshape(RANK // HALF, HALF),
    )


def solution(mesh):
    placed = (P("slab", "col", None), P(), P(), P(), P())
    return jax.shard_map(
        on_device, mesh=mesh, in_specs=placed, out_specs=P("col", "slab", None), check_vma=False
    )
```
